256 devices in a mesh: gx: 8 (over z), gy: 16 (over y, x), gz: 2 (over core).
Axes of the slice: x: 4, y: 4, z: 8, core: 2. Of those that a mesh axis runs over, the one named last changes fastest.
Arguments:
- adjoint_rhs: float32 [2, 128, 256, 2048], P(None, 'gx', 'gy', 'gz'), may hold values from -8 to 8
- conductance: float32 [128, 256, 2048], P('gx', 'gy', 'gz'), may hold values from 0.2 to 5
- phase: int32 [128, 256, 2048], P('gx', 'gy', 'gz'), may hold values from 0 to 2
- particle_rhs: float32 [1200, 8192], P(None, ('gx', 'gy', 'gz')), may hold values from -8 to 8
- diffusion_rate: float32 [8, 8192], P(None, ('gx', 'gy', 'gz')), may hold values from 0.2 to 5
- exchange_rate: float32 [8, 8192], P(None, ('gx', 'gy', 'gz')), may hold values from 0.3 to 3
- record_voxel: int32 [8, 16, 2, 3, 512], P('gx', 'gy', 'gz'), may hold values from 0 to 262143, as said below
- record_slot: int32 [8, 16, 2, 3, 512], P('gx', 'gy', 'gz'), may hold values from 0 to 255, as said below
- record_weight: float32 [8, 16, 2, 3, 512], P('gx', 'gy', 'gz'), may hold values from 0 to 1, as said below
Outputs:
- voxel_adjoint: float32 [2, 128, 256, 2048], P(None, 'gx', 'gy', 'gz')
- shell_adjoint: float32 [1200, 8192], P(None, ('gx', 'gy', 'gz'))
The draws below stay inside these ranges and needn't reach their ends.
Inputs may be any that keep to these rules, and one draw needn't show every extreme that they name: `record_voxel`: index within the brick of a voxel; for block 0 (2) a voxel among the first (last) 4 layers along the second dimension, at least one layer. `record_slot`: class times 32 plus column on the brick named by the fourth index. `record_weight`: zero in unused slots and in blocks whose brick lies outside the grid; the used slots of each block of 512 come first; every brick fills all 512 slots of one of its blocks.
All inputs are finite; a program needn't handle non-finite values.
Results may differ from the reference program's by a relative error of at most 0.0001.
Values sent between devices are 32-bit elements; how exact they have to be, the bound alone decides.
A program may use at most 128 MiB of HBM per device.

```python
import math
import jax
import jax.numpy as jnp

BX = 16
BY = 16
BZ = 1024
PC = 32
CLASSES = 8
SHELL_ROWS = 1200
FIELDS = 2
ITERS = 4
BRICKS_X = 8
BRICKS_Y = 16
BRICKS_Z = 2
NX = 128
NY = 256
NZ = 2048
PCOLS = 8192
CAP = 512
N_GX = 8
N_GY = 16
N_GZ = 2


def record_live(key):
    layout_key = jax.random.fold_in(key, 7)
    key_level, key_raw, key_shift = jax.random.split(layout_key, 3)
    level = jax.random.randint(key_level, (BRICKS_X, BRICKS_Y, BRICKS_Z, 1), 2, 6)
    raw = jax.random.randint(key_raw, (BRICKS_X, BRICKS_Y, BRICKS_Z, 3), 0, CAP + 1)
    counts = jnp.minimum(CAP, raw * level // 4)
    own = jnp.arange(BRICKS_Y)[None, :, None, None]
    offset = jnp.arange(3)[None, None, None, :]
    peer = own + offset - 1
    valid = (peer >= 0) & (peer < BRICKS_Y)
    shift = jax.random.randint(key_shift, (BRICKS_X, BRICKS_Y, BRICKS_Z, 1), 0, 3)
    shift_peer = own + shift - 1
    shift_ok = (shift_peer >= 0) & (shift_peer < BRICKS_Y)
    full = jnp.where(shift_ok, shift, 1)
    counts = jnp.where(offset == full, CAP, counts)
    counts = jnp.where(valid, counts, 0)
    return jnp.arange(CAP)[None, None, None, None, :] < counts[..., None]


def draw_record_voxel(key, part):
    shape = (BRICKS_X, BRICKS_Y, BRICKS_Z, 3, CAP)
    key_i, key_j, key_k, key_rim = jax.random.split(jax.random.fold_in(key, 11), 4)
    rim = max(1, BY // 4)
    row_i = jax.random.randint(key_i, shape, 0, BX)
    row_k = jax.random.randint(key_k, shape, 0, BZ)
    anywhere = jax.random.randint(key_j, shape, 0, BY)
    near = jax.random.randint(key_rim, shape, 0, rim)
    offset = jnp.arange(3)[None, None, None, :, None]
    row_j = jnp.where(offset == 0, near, jnp.where(offset == 2, BY - 1 - near, anywhere))
    return (row_i * (BY * BZ) + row_j * BZ + row_k).astype(jnp.int32)


def draw_record_slot(key, part):
    return jax.random.randint(jax.random.fold_in(key, 13), (BRICKS_X, BRICKS_Y, BRICKS_Z, 3, CAP), 0, CLASSES * PC).astype(jnp.int32)


def draw_record_weight(key, part):
    live = record_live(key)
    shape = (BRICKS_X, BRICKS_Y, BRICKS_Z, 3, CAP)
    values = jax.random.uniform(jax.random.fold_in(key, 17), shape, jnp.float32, 0.2, 1.0)
    return jnp.where(live, values, 0.0).astype(jnp.float32)


def set_ends(entries, stream_key, least, high):
    index_at = [jax.random.randint(jax.random.fold_in(stream_key, axis), (), 0, length) for axis, length in enumerate(entries.shape)]
    main_axis = entries.shape.index(max(entries.shape))
    next_to = index_at[:main_axis] + [(index_at[main_axis] + 1) % entries.shape[main_axis]] + index_at[main_axis + 1:]
    return entries.at[tuple(index_at)].set(least).at[tuple(next_to)].set(high)


def block_levels(key, extent, cuts, smallest, high):
    gain, own = 1.0, jax.random.fold_in(key, 6)
    for dim, parts in cuts:
        steps = jnp.exp(jax.random.uniform(jax.random.fold_in(own, dim), (parts,), jnp.float32, smallest / len(cuts), high / len(cuts)))
        gain = gain * jnp.repeat(steps, extent[dim] // parts).reshape([-1 if axis == dim else 1 for axis in range(len(extent))])
    return gain


def bell_draw(own_key, extent, width, reach, shards=(), kind=jnp.bfloat16):
    entries = width * jax.random.normal(own_key, extent, jnp.float32)
    if shards:
        entries = entries * block_levels(own_key, extent, shards, -0.22, 0.18)
    return jnp.clip(entries, -reach, reach).astype(kind)


def setup_inputs(seed: int = 0) -> dict:
    key_list = jax.random.split(jax.random.key(seed), 10)
    adjoint_rhs = bell_draw(key_list[0], (FIELDS, NX, NY, NZ), 1.0, 8.0, ((1, 8), (2, 16), (3, 2)), jnp.float32)
    conductance = jnp.clip(jnp.exp(math.log(5.0) - 3.218876 * jax.random.uniform(key_list[1], (NX, NY, NZ), jnp.float32) ** block_levels(key_list[1], (NX, NY, NZ), ((0, 8), (1, 16), (2, 2)), -0.2, 0.2)), 0.2, 5.0)
    phase = set_ends(jax.random.randint(key_list[2], (NX, NY, NZ), 0, 3), jax.random.fold_in(key_list[2], 1), 0, 2).astype(jnp.int32)
    particle_rhs = bell_draw(key_list[3], (SHELL_ROWS, PCOLS), 1.0, 8.0, ((1, 256),), jnp.float32)
    diffusion_rate = jnp.clip(jnp.exp(math.log(5.0) - 3.218876 * jax.random.uniform(key_list[4], (CLASSES, PCOLS), jnp.float32) ** block_levels(key_list[4], (CLASSES, PCOLS), ((1, 256),), -0.2, 0.2)), 0.2, 5.0)
    exchange_rate = jnp.clip(jnp.exp(math.log(3.0) - 2.3025851 * jax.random.uniform(key_list[5], (CLASSES, PCOLS), jnp.float32) ** block_levels(key_list[5], (CLASSES, PCOLS), ((1, 256),), -0.2, 0.2)), 0.3, 3.0)
    record_voxel = draw_record_voxel(jax.random.fold_in(key_list[9], 71), 0)
    record_slot = draw_record_slot(jax.random.fold_in(key_list[9], 71), 0)
    record_weight = draw_record_weight(jax.random.fold_in(key_list[9], 71), 0)
    return dict(adjoint_rhs=adjoint_rhs, conductance=conductance, phase=phase, particle_rhs=particle_rhs, diffusion_rate=diffusion_rate, exchange_rate=exchange_rate, record_voxel=record_voxel, record_slot=record_slot, record_weight=record_weight)


shell_counts = (64, 80, 96, 128, 160, 192, 224, 256)
conduct_potential = (1.0, 0.1, 0.5)
conduct_salt = (1.0, 0.05, 0.3)
mass_potential = (1.0, 0.5, 0.8)
mass_salt = (1.0, 2.0, 1.5)
coupling_weights = (1.0, 0.5)


def phase_value(phase, values):
    return jnp.where(phase == 0, values[0], jnp.where(phase == 1, values[1], values[2]))


def neighbours(padded):
    return [padded[:, 2:, 1:-1, 1:-1], padded[:, :-2, 1:-1, 1:-1],
            padded[:, 1:-1, 2:, 1:-1], padded[:, 1:-1, :-2, 1:-1],
            padded[:, 1:-1, 1:-1, 2:], padded[:, 1:-1, 1:-1, :-2]]


def shell_geometry(count):
    faces = jnp.arange(count + 1).astype(jnp.float32)
    area = jnp.where(faces < count, (faces / count) ** 2, 0.0)
    shells = jnp.arange(count).astype(jnp.float32)
    volume = (3.0 * shells * shells + 3.0 * shells + 1.0) / (3.0 * count * count)
    return area, volume


def particle_update(block, rhs_block, rate, gamma, surf, area, volume, diagonal):
    scaled = block / volume[:, None]
    padded = jnp.pad(scaled, ((1, 1), (0, 0)))
    inner = area[1:, None] * padded[2:] + area[:-1, None] * padded[:-2]
    numer = rhs_block + rate[None, :] * inner
    numer = numer.at[-1].add(gamma * surf)
    return numer / diagonal


def reference(adjoint_rhs, conductance, phase, particle_rhs, diffusion_rate, exchange_rate, record_voxel, record_slot, record_weight):
    kappa = conductance[None] * jnp.stack([phase_value(phase, conduct_potential), phase_value(phase, conduct_salt)])
    mass = jnp.stack([phase_value(phase, mass_potential), phase_value(phase, mass_salt)])
    padded_k = jnp.pad(kappa, ((0, 0), (1, 1), (1, 1), (1, 1)))
    coefs = [2.0 * kappa * other / (kappa + other) for other in neighbours(padded_k)]
    brick_x = jnp.arange(N_GX, dtype=jnp.int32)[:, None, None, None, None]
    brick_y = jnp.arange(N_GY, dtype=jnp.int32)[None, :, None, None, None]
    brick_z = jnp.arange(N_GZ, dtype=jnp.int32)[None, None, :, None, None]
    offset = jnp.arange(3, dtype=jnp.int32)[None, None, None, :, None]
    peer = jnp.clip(brick_y + offset - 1, 0, N_GY - 1)
    row_i = record_voxel // (BY * BZ)
    row_j = (record_voxel // BZ) % BY
    row_k = record_voxel % BZ
    global_voxel = (((brick_x * BX + row_i) * NY + brick_y * BY + row_j) * NZ + brick_z * BZ + row_k).reshape(-1)
    owner = (brick_x * N_GY + peer) * N_GZ + brick_z
    particle_flat = ((record_slot // PC) * PCOLS + owner * PC + record_slot % PC).reshape(-1)
    weight = record_weight.reshape(-1)
    total_cells = NX * NY * NZ
    voxel_weight = jnp.zeros((total_cells,), jnp.float32).at[global_voxel].add(weight).reshape(NX, NY, NZ)
    particle_weight = jnp.zeros((CLASSES * PCOLS,), jnp.float32).at[particle_flat].add(weight).reshape(CLASSES, PCOLS)
    coupling = jnp.array(coupling_weights, jnp.float32)[:, None, None, None]
    diag_x = mass + coupling * voxel_weight[None] + sum(coefs)
    starts = [sum(shell_counts[:index]) for index in range(len(shell_counts))]
    geometry = []
    blocks = []
    for index, count in enumerate(shell_counts):
        area, volume = shell_geometry(count)
        diagonal = 1.0 + diffusion_rate[index][None, :] * ((area[1:] + area[:-1]) / volume)[:, None]
        diagonal = diagonal.at[-1].add(exchange_rate[index] * (coupling_weights[0] + coupling_weights[1]) * particle_weight[index])
        geometry.append((area, volume, diagonal))
        blocks.append(particle_rhs[starts[index]:starts[index] + count] / diagonal)
    voxel_adj = adjoint_rhs / diag_x
    for step in range(ITERS):
        last = jnp.stack([block[-1] for block in blocks]).reshape(-1)
        back = jnp.zeros((total_cells,), jnp.float32).at[global_voxel].add(weight * last[particle_flat]).reshape(NX, NY, NZ)
        flat_x = voxel_adj.reshape(FIELDS, -1)
        mixed = coupling_weights[0] * flat_x[0] + coupling_weights[1] * flat_x[1]
        surf = jnp.zeros((CLASSES * PCOLS,), jnp.float32).at[particle_flat].add(weight * mixed[global_voxel]).reshape(CLASSES, PCOLS)
        padded = jnp.pad(voxel_adj, ((0, 0), (1, 1), (1, 1), (1, 1)))
        near_sum = sum(coef * other for coef, other in zip(coefs, neighbours(padded)))
        new_x = (adjoint_rhs + near_sum + coupling * back[None]) / diag_x
        new_blocks = []
        for index, count in enumerate(shell_counts):
            area, volume, diagonal = geometry[index]
            new_blocks.append(particle_update(blocks[index], particle_rhs[starts[index]:starts[index] + count],
                                              diffusion_rate[index], exchange_rate[index], surf[index], area, volume, diagonal))
        voxel_adj = new_x
        blocks = new_blocks
    return voxel_adj, jnp.concatenate(blocks, axis=0)
```

```python
import jax
import jax.numpy as jnp
from jax import lax
from jax.experimental import pallas as pl
from jax.experimental.pallas import tpu as pltpu
from jax.sharding import PartitionSpec as P

ITERS = 4
shell_counts = (64, 80, 96, 128, 160, 192, 224, 256)
shell_starts = tuple(sum(shell_counts[:i]) for i in range(8))
conduct = ((1.0, 0.1, 0.5), (1.0, 0.05, 0.3))
masses = ((1.0, 0.5, 0.8), (1.0, 2.0, 1.5))
coupling = (1.0, 0.5)
groups = ((0, 128), (128, 256))
PACKED = 384

F32 = jnp.float32
BF16 = jnp.bfloat16
MESH = pl.DeviceIdType.MESH
N = 16


def pick(phase, values):
    return jnp.where(phase == 0, values[0], jnp.where(phase == 1, values[1], values[2]))


def inverse(d):
    r = pl.reciprocal(d, approx=True)
    r = r * (2.0 - d * r)
    return r * (2.0 - d * r)


def face(a, b):
    return 2.0 * a * b * inverse(a + b)


def split(v):
    hi = v.astype(BF16)
    lo = (v - hi.astype(F32)).astype(BF16)
    return hi, lo


def ahead(x, row, lane, sub):
    t = jnp.where(lane == 0, pltpu.roll(x, 7, 0), x)
    t = jnp.where((lane == 0) & (sub == 7), row, t)
    return pltpu.roll(t, 127, 1)


def behind(x, row, lane, sub):
    t = jnp.where(lane == 127, pltpu.roll(x, 1, 0), x)
    t = jnp.where((lane == 127) & (sub == 0), row, t)
    return pltpu.roll(t, 1, 1)


def dot(a, b):
    return jnp.dot(a, b, preferred_element_type=F32)


def dot_t(a, b):
    return lax.dot_general(a, b, (((1,), (1,)), ((), ())), preferred_element_type=F32)


def kernel(
    rhs_h, cond_h, phase_h, prhs_h, rate_ref, gamma_ref, vox_ref, slot_ref, wgt_ref,
    xo_h, yo_ref,
    rhs, cond, phase, prhs,
    kap, fx, fy, fzp, fzm, inv, xb, hx, hy, hz, cx, cy,
    back, m1, m0, m2, r1, r0, r2, r1t, r0t, r2t, sel, wc, q_scr, vc, rec, rect,
    yb, ydn, yup, yrhs, gsurf, lsend, lrecv, ssend, srecv,
    in_sem, out_sem, send_sem, recv_sem,
):
    gx = lax.axis_index("gx")
    gy = lax.axis_index("gy")
    gz = lax.axis_index("gz")
    nx, ny = lax.axis_size("gx"), lax.axis_size("gy")
    x_dn = {"gx": lax.rem(gx + nx - 1, nx)}
    x_up = {"gx": lax.rem(gx + 1, nx)}
    y_dn = {"gy": lax.rem(gy + ny - 1, ny)}
    y_up = {"gy": lax.rem(gy + 1, ny)}
    z_other = {"gz": 1 - gz}
    z_row = 7 * (1 - gz)

    copies = [
        pltpu.make_async_copy(src, dst, in_sem.at[n])
        for n, (src, dst) in enumerate(
            ((cond_h, cond), (phase_h, phase), (rhs_h, rhs), (prhs_h, prhs))
        )
    ]
    for copy in copies:
        copy.start()

    lsend[...] = jnp.zeros((8, 128), F32)
    ssend[...] = jnp.zeros((2, 8, 128), F32)
    barrier = pltpu.get_barrier_semaphore()
    for peer in (x_dn, x_up, y_dn, y_up, z_other):
        pl.semaphore_signal(barrier, inc=1, device_id=peer, device_id_type=MESH)
    pl.semaphore_wait(barrier, 5)

    def remote(src, dst, e, n, peer):
        return pltpu.make_async_remote_copy(
            src_ref=src, dst_ref=dst, send_sem=send_sem.at[e, n], recv_sem=recv_sem.at[e, n],
            device_id=peer, device_id_type=MESH,
        )

    def halo_copies(src, e):
        return (
            remote(src.at[:, 0], hx.at[e, 1], e, 0, x_dn),
            remote(src.at[:, N - 1], hx.at[e, 0], e, 1, x_up),
            remote(src.at[:, :, 0], hy.at[e, 1], e, 2, y_dn),
            remote(src.at[:, :, N - 1], hy.at[e, 0], e, 3, y_up),
            remote(src.at[:, :, :, z_row], hz.at[e], e, 4, z_other),
        )

    def sum_copies(e):
        return (
            remote(ssend.at[0], srecv.at[e, 1], e, 5, y_dn),
            remote(ssend.at[1], srecv.at[e, 0], e, 6, y_up),
        )

    def last_copies(e):
        return (
            remote(lsend, lrecv.at[e, 1], e, 7, y_dn),
            remote(lsend, lrecv.at[e, 0], e, 8, y_up),
        )

    lane = lax.broadcasted_iota(jnp.int32, (8, 128), 1)
    sub = lax.broadcasted_iota(jnp.int32, (8, 128), 0)

    copies[0].wait()
    copies[1].wait()

    def kappa_plane(i, _):
        for j in range(N):
            c, p = cond[i, j], phase[i, j]
            for f in range(2):
                kap[f, i, j] = c * pick(p, conduct[f])
        return 0

    lax.fori_loop(0, N, kappa_plane, 0)
    kap_copies = halo_copies(kap, 0)
    for copy in kap_copies:
        copy.start()

    rec[...] = jnp.zeros((128, 128), F32)
    for o in range(3):
        for q in range(4):
            at = pl.ds(128 * q, 128)
            rec[pl.ds(o * 4 + q, 1), :] = vox_ref[pl.ds(o, 1), at].astype(F32)
            rec[pl.ds(12 + o * 4 + q, 1), :] = slot_ref[pl.ds(o, 1), at].astype(F32)
            rec[pl.ds(24 + o * 4 + q, 1), :] = wgt_ref[pl.ds(o, 1), at]
    rect[...] = jnp.transpose(rec[...])

    for o, ref, width in ((0, r0, 512), (1, r1, 2048), (2, r2, 512)):
        for q in range(4):
            n = o * 4 + q
            voxel = rect[:, n : n + 1]
            slot = rect[:, 12 + n : 13 + n]
            weight = rect[:, 24 + n : 25 + n]
            row = jnp.floor(voxel * (1.0 / 128.0))
            at_lane = voxel - row * 128.0
            if o != 1:
                plane = jnp.floor(row * (1.0 / 128.0))
                row = row - plane * 96.0 - (96.0 if o == 2 else 0.0)
            lanes = lax.broadcasted_iota(jnp.int32, (128, 128), 1).astype(F32)
            wc[o, pl.ds(128 * q, 128), :] = jnp.where(lanes == at_lane, weight, 0.0)
            for h in range(2):
                hit = (lanes + 128.0 * h) == slot
                sel[o, pl.ds(128 * q, 128), pl.ds(128 * h, 128)] = jnp.where(hit, 1.0, 0.0).astype(BF16)
            for h in range(width // 128):
                hit = (lanes + 128.0 * h) == row
                ref[pl.ds(128 * q, 128), pl.ds(128 * h, 128)] = jnp.where(hit, 1.0, 0.0).astype(BF16)

    for o, ref, width in ((0, r0t, 512), (1, r1t, 2048), (2, r2t, 512)):
        row = lax.shift_right_logical(vox_ref[pl.ds(o, 1), :], 7)
        if o != 1:
            row = row - lax.shift_right_logical(row, 7) * 96 - (96 if o == 2 else 0)

        def fill(c, _, ref=ref, row=row):
            at = pl.multiple_of(c * 64, 64)
            down = lax.broadcasted_iota(jnp.int32, (64, 512), 0) + at
            ref[pl.ds(at, 64), :] = jnp.where(down == row, 1.0, 0.0).astype(BF16)
            return 0

        lax.fori_loop(0, width // 64, fill, 0)

    def particle_sums(src):
        sums = []
        for o in range(3):
            both = jnp.concatenate(split(src[o]), axis=1)
            per_record = dot_t(jnp.ones((16, 256), BF16), both)
            parts = dot(jnp.concatenate(split(per_record), axis=0), sel[o])
            sums.append(parts[0:1] + parts[16:17])
        return sums

    def send_sums(sums, e):
        for d, s in ((0, sums[0]), (1, sums[2])):
            ssend[d, 0:1, :] = s[:, :128]
            ssend[d, 1:2, :] = s[:, 128:]
        for copy in sum_copies(e):
            copy.start()
        return sums[1]

    def to_voxels():
        full = dot(r1t[...], vc[1])
        back[...] = full[:, :128] + full[:, 128:]
        for o, ref, base in ((0, r0t, 0), (2, r2t, 96)):
            part = dot(ref[...], vc[o])
            part = part[:, :128] + part[:, 128:]
            for i in range(N):
                back[pl.ds(i * 128 + base, 32), :] += part[i * 32 : i * 32 + 32]

    own_weight = send_sums(particle_sums(wc), 0)
    for o in range(3):
        hi, lo = split(wc[o])
        vc[o, :, 0:128] = hi
        vc[o, :, 128:256] = lo
    to_voxels()

    kap_copies[4].wait_recv()
    first_z = (gz == 0).astype(F32)

    fx[:, 0] = jnp.zeros((2, N, 8, 128), F32)
    fx[:, N] = jnp.zeros((2, N, 8, 128), F32)

    def face_plane(i, _):
        below = jnp.maximum(i - 1, 0)
        not_first = (i > 0).astype(F32)
        for f in range(2):
            for j in range(N):
                k = kap[f, i, j]
                row = jnp.broadcast_to(hz[0, f, i, pl.ds(j, 1), :], (8, 128))
                fx[f, i, j] = not_first * face(k, kap[f, below, j])
                if j:
                    fy[f, i, j] = face(k, kap[f, i, j - 1])
                nxt = ahead(k, row * first_z, lane, sub)
                up = face(k, nxt)
                fzp[f, i, j] = up
                prev = behind(k, row * (1.0 - first_z), lane, sub)
                fzm[f, i, j] = face(k, prev)
        return 0

    lax.fori_loop(0, N, face_plane, 0)

    def diag_plane(i, _):
        for f in range(2):
            for j in range(N):
                d = pick(phase[i, j], masses[f]) + coupling[f] * back[pl.ds(pl.multiple_of(i * 128 + j * 8, 8), 8), :]
                d = d + fx[f, i, j] + fx[f, i + 1, j] + fzp[f, i, j] + fzm[f, i, j]
                if j:
                    d = d + fy[f, i, j]
                if j < N - 1:
                    d = d + fy[f, i, j + 1]
                inv[f, i, j] = d
        return 0

    lax.fori_loop(0, N, diag_plane, 0)

    for copy in kap_copies[:4]:
        copy.wait_recv()
    inside = (
        (gx > 0).astype(F32), (gx < nx - 1).astype(F32),
        (gy > 0).astype(F32), (gy < ny - 1).astype(F32),
    )

    def rim_faces(n, _):
        for f in range(2):
            for d, at in ((0, 0), (1, N - 1)):
                c = inside[d] * face(kap[f, at, n], hx[0, d, f, n])
                cx[d, f, n] = c
                inv[f, at, n] += c
            for d, at in ((0, 0), (1, N - 1)):
                c = inside[2 + d] * face(kap[f, n, at], hy[0, d, f, n])
                cy[d, f, n] = c
                inv[f, n, at] += c
        return 0

    lax.fori_loop(0, N, rim_faces, 0)
    copies[2].wait()

    def start_plane(i, _):
        for f in range(2):
            for j in range(N):
                v = inverse(inv[f, i, j])
                inv[f, i, j] = v
                xb[0, f, i, j] = rhs[f, i, j] * v
        return 0

    lax.fori_loop(0, N, start_plane, 0)

    def rim_scale(n, _):
        for f in range(2):
            for d, at in ((0, 0), (1, N - 1)):
                cx[d, f, n] *= inv[f, at, n]
                cy[d, f, n] *= inv[f, n, at]
        return 0

    lax.fori_loop(0, N, rim_scale, 0)

    copies[3].wait()
    yb[0] = jnp.zeros((PACKED, 128), F32)
    rates = []
    for g, (base, rows) in enumerate(groups):
        for c in range(4):
            cls = 4 * g + c
            count = shell_counts[cls]
            yb[0, pl.ds(base + rows - count, count), 32 * c : 32 * c + 32] = prhs[
                pl.ds(shell_starts[cls], count), :
            ]
        rates.append(
            [
                jnp.concatenate([ref[4 * g + c : 4 * g + c + 1, :] for c in range(4)], axis=1)
                for ref in (rate_ref, gamma_ref)
            ]
        )
    for copy in sum_copies(0):
        copy.wait_recv()
    for g, (base, rows) in enumerate(groups):
        rate, gamma = rates[g]
        sums = own_weight[:, 128 * g : 128 * g + 128] + srecv[0, 0, g : g + 1, :] + srecv[0, 1, g : g + 1, :]
        down = lax.broadcasted_iota(jnp.int32, (rows, 128), 0)
        part = lax.broadcasted_iota(jnp.int32, (rows, 128), 1) // 32
        cnt = shell_counts[4 * g : 4 * g + 4]
        count = jnp.where(part == 0, cnt[0], jnp.where(part == 1, cnt[1], jnp.where(part == 2, cnt[2], cnt[3])))
        s = (down - (rows - count)).astype(F32)
        live = s >= 0.0
        last = down == rows - 1
        count = count.astype(F32)
        unit = inverse(count)
        lower = jnp.where(live, (s * unit) * (s * unit), 0.0)
        upper = jnp.where(live & ~last, ((s + 1.0) * unit) * ((s + 1.0) * unit), 0.0)
        cube = 3.0 * count * count

        def over_volume(s):
            return cube * inverse(3.0 * s * s + 3.0 * s + 1.0)

        d = 1.0 + rate * ((upper + lower) * over_volume(s))
        d = d + jnp.where(last, gamma * (coupling[0] + coupling[1]) * sums, 0.0)
        d = inverse(d)
        at = pl.ds(base, rows)
        ydn[at, :] = rate * lower * over_volume(s - 1.0) * d
        yup[at, :] = rate * upper * over_volume(s + 1.0) * d
        y = yb[0, at, :] * d
        yrhs[at, :] = y
        yb[0, at, :] = y
        gsurf[pl.ds(g, 1), :] = gamma * d[rows - 1 : rows]

    for copy in kap_copies + sum_copies(0):
        copy.wait_send()

    def iteration(t, _):
        e = t + 1
        cur = lax.rem(t, 2)
        new = 1 - cur
        x = xb.at[cur]
        xn = xb.at[new]
        halos = halo_copies(x, e)
        for copy in halos:
            copy.start()
        own_last = jnp.concatenate([yb[0, 127:128, :], yb[0, 383:384, :]], axis=1)
        lsend[0:1, :] = yb[0, 127:128, :]
        lsend[1:2, :] = yb[0, 383:384, :]
        lasts = last_copies(e)
        for copy in lasts:
            copy.start()

        def mix(i, _):
            for jp in range(N // 2):
                at = pl.ds(2 * jp, 2)
                v = coupling[0] * x[0, i, at] + coupling[1] * x[1, i, at]
                hi, lo = split(v.reshape(16, 128))
                targets = [(m1, i * 128 + jp * 16)]
                if jp < 2:
                    targets.append((m0, i * 32 + jp * 16))
                if jp >= 6:
                    targets.append((m2, i * 32 + (jp - 6) * 16))
                for ref, start in targets:
                    rows = pl.ds(pl.multiple_of(start, 16), 16)
                    ref[rows, 0:128] = hi
                    ref[rows, 128:256] = lo
            return 0

        lax.fori_loop(0, N, mix, 0)
        for o, ref, m in ((0, r0, m0), (2, r2, m2), (1, r1, m1)):
            got = dot(ref[...], m[...])
            q_scr[o] = (got[:, :128] + got[:, 128:]) * wc[o]
        own_sum = send_sums(particle_sums(q_scr), e)

        for copy in lasts:
            copy.wait_recv()
        for o in range(3):
            if o == 1:
                table = own_last
            else:
                table = jnp.concatenate([lrecv[e, o // 2, 0:1, :], lrecv[e, o // 2, 1:2, :]], axis=1)
            hi, lo = split(table)
            table = jnp.concatenate(
                [jnp.broadcast_to(hi, (128, 256)), jnp.broadcast_to(lo, (128, 256))], axis=0
            )
            got = dot_t(sel[o], table)
            hi, lo = split((got[:, :128] + got[:, 128:]) * wc[o])
            vc[o, :, 0:128] = hi
            vc[o, :, 128:256] = lo
        to_voxels()

        halos[4].wait_recv()

        def plane(i, _):
            below = jnp.maximum(i - 1, 0)
            above = jnp.minimum(i + 1, N - 1)
            for j in range(N):
                b = back[pl.ds(pl.multiple_of(i * 128 + j * 8, 8), 8), :]
                for f in range(2):
                    v = x[f, i, j]
                    row = jnp.broadcast_to(hz[e, f, i, pl.ds(j, 1), :], (8, 128))
                    acc = rhs[f, i, j] + coupling[f] * b
                    acc += fx[f, i, j] * x[f, below, j]
                    acc += fx[f, i + 1, j] * x[f, above, j]
                    if j:
                        acc += fy[f, i, j] * x[f, i, j - 1]
                    if j < N - 1:
                        acc += fy[f, i, j + 1] * x[f, i, j + 1]
                    acc += fzp[f, i, j] * ahead(v, row, lane, sub)
                    acc += fzm[f, i, j] * behind(v, row, lane, sub)
                    xn[f, i, j] = acc * inv[f, i, j]
            return 0

        lax.fori_loop(0, N, plane, 0)

        for copy in sum_copies(e):
            copy.wait_recv()
        y = yb[0]
        y = yrhs[...] + ydn[...] * pltpu.roll(y, 1, 0) + yup[...] * pltpu.roll(y, PACKED - 1, 0)
        yb[0] = y
        for g, row in ((0, 127), (1, 383)):
            sums = own_sum[:, 128 * g : 128 * g + 128] + srecv[e, 0, g : g + 1, :] + srecv[e, 1, g : g + 1, :]
            yb[0, row : row + 1, :] += gsurf[pl.ds(g, 1), :] * sums

        for copy in halos[:4]:
            copy.wait_recv()

        def rim(n, _):
            for f in range(2):
                for d, at in ((0, 0), (1, N - 1)):
                    xn[f, at, n] += cx[d, f, n] * hx[e, d, f, n]
                for d, at in ((0, 0), (1, N - 1)):
                    xn[f, n, at] += cy[d, f, n] * hy[e, d, f, n]
            return 0

        lax.fori_loop(0, N, rim, 0)
        for copy in halos + lasts + sum_copies(e):
            copy.wait_send()
        return 0

    lax.fori_loop(0, ITERS, iteration, 0)

    out = pltpu.make_async_copy(xb.at[0], xo_h, out_sem)
    out.start()
    for g, (base, rows) in enumerate(groups):
        for c in range(4):
            cls = 4 * g + c
            count = shell_counts[cls]
            yo_ref[pl.ds(shell_starts[cls], count), :] = yb[
                0, pl.ds(base + rows - count, count), 32 * c : 32 * c + 32
            ]
    out.wait()


def shards(
    adjoint_rhs, conductance, phase, particle_rhs, diffusion_rate, exchange_rate,
    record_voxel, record_slot, record_weight,
):
    vmem = pl.BlockSpec(memory_space=pltpu.VMEM)
    hbm = pl.BlockSpec(memory_space=pl.ANY)
    field = (2, N, N, 8, 128)
    col = (8, 128)
    scratch = [
        pltpu.VMEM(field, F32),
        pltpu.VMEM(field[1:], F32),
        pltpu.VMEM(field[1:], jnp.int32),
        pltpu.VMEM((1200, 32), F32),
        pltpu.VMEM(field, F32),
        pltpu.VMEM((2, N + 1, N, *col), F32),
        pltpu.VMEM(field, F32),
        pltpu.VMEM(field, F32),
        pltpu.VMEM(field, F32),
        pltpu.VMEM(field, F32),
        pltpu.VMEM((2, *field), F32),
        pltpu.VMEM((5, 2, 2, N, *col), F32),
        pltpu.VMEM((5, 2, 2, N, *col), F32),
        pltpu.VMEM((5, 2, N, N, 128), F32),
        pltpu.VMEM((2, 2, N, *col), F32),
        pltpu.VMEM((2, 2, N, *col), F32),
        pltpu.VMEM((2048, 128), F32),
        pltpu.VMEM((2048, 256), BF16),
        pltpu.VMEM((512, 256), BF16),
        pltpu.VMEM((512, 256), BF16),
        pltpu.VMEM((512, 2048), BF16),
        pltpu.VMEM((512, 512), BF16),
        pltpu.VMEM((512, 512), BF16),
        pltpu.VMEM((2048, 512), BF16),
        pltpu.VMEM((512, 512), BF16),
        pltpu.VMEM((512, 512), BF16),
        pltpu.VMEM((3, 512, 256), BF16),
        pltpu.VMEM((3, 512, 128), F32),
        pltpu.VMEM((3, 512, 128), F32),
        pltpu.VMEM((3, 512, 256), BF16),
        pltpu.VMEM((128, 128), F32),
        pltpu.VMEM((128, 128), F32),
        pltpu.VMEM((1, PACKED, 128), F32),
        pltpu.VMEM((PACKED, 128), F32),
        pltpu.VMEM((PACKED, 128), F32),
        pltpu.VMEM((PACKED, 128), F32),
        pltpu.VMEM(col, F32),
        pltpu.VMEM(col, F32),
        pltpu.VMEM((5, 2, *col), F32),
        pltpu.VMEM((2, *col), F32),
        pltpu.VMEM((5, 2, *col), F32),
        pltpu.SemaphoreType.DMA((4,)),
        pltpu.SemaphoreType.DMA,
        pltpu.SemaphoreType.DMA((5, 9)),
        pltpu.SemaphoreType.DMA((5, 9)),
    ]
    x, y = pl.pallas_call(
        kernel,
        out_shape=(
            jax.ShapeDtypeStruct(field, F32),
            jax.ShapeDtypeStruct((1200, 32), F32),
        ),
        in_specs=[hbm, hbm, hbm, hbm, vmem, vmem, vmem, vmem, vmem],
        out_specs=(hbm, vmem),
        scratch_shapes=scratch,
        compiler_params=pltpu.CompilerParams(
            collective_id=0, has_side_effects=True, vmem_limit_bytes=56 * 1024 * 1024
        ),
    )(
        adjoint_rhs.reshape(field),
        conductance.reshape(field[1:]),
        phase.reshape(field[1:]),
        particle_rhs,
        diffusion_rate,
        exchange_rate,
        record_voxel.reshape(3, 512),
        record_slot.reshape(3, 512),
        record_weight.reshape(3, 512),
    )
    return x.reshape(2, N, N, 1024), y


def solution(mesh):
    grid = P("gx", "gy", "gz")
    parts = P(None, ("gx", "gy", "gz"))
    return jax.shard_map(
        shards,
        mesh=mesh,
        in_specs=(P(None, "gx", "gy", "gz"), grid, grid, parts, parts, parts, grid, grid, grid),
        out_specs=(P(None, "gx", "gy", "gz"), parts),
        check_vma=False,
    )
```

```python
import jax
import jax.numpy as jnp
from jax import lax
from jax.experimental import pallas as pl
from jax.experimental.pallas import tpu as pltpu
from jax.sharding import PartitionSpec as P

ITERS = 4
shell_counts = (64, 80, 96, 128, 160, 192, 224, 256)
shell_starts = tuple(sum(shell_counts[:i]) for i in range(8))
conduct = ((1.0, 0.1, 0.5), (1.0, 0.05, 0.3))
masses = ((1.0, 0.5, 0.8), (1.0, 2.0, 1.5))
coupling = (1.0, 0.5)
groups = ((0, 128), (128, 256))
PACKED = 384

F32 = jnp.float32
BF16 = jnp.bfloat16
MESH = pl.DeviceIdType.MESH
N = 16


def pick(phase, values):
    return jnp.where(phase == 0, values[0], jnp.where(phase == 1, values[1], values[2]))


def inverse(d):
    r = pl.reciprocal(d, approx=True)
    r = r * (2.0 - d * r)
    return r * (2.0 - d * r)


def face(a, b):
    return 2.0 * a * b * inverse(a + b)


def split(v):
    hi = v.astype(BF16)
    lo = (v - hi.astype(F32)).astype(BF16)
    return hi, lo


def ahead(x, row, lane, sub):
    t = jnp.where(lane == 0, pltpu.roll(x, 7, 0), x)
    t = jnp.where((lane == 0) & (sub == 7), row, t)
    return pltpu.roll(t, 127, 1)


def behind(x, row, lane, sub):
    t = jnp.where(lane == 127, pltpu.roll(x, 1, 0), x)
    t = jnp.where((lane == 127) & (sub == 0), row, t)
    return pltpu.roll(t, 1, 1)


def dot(a, b):
    return jnp.dot(a, b, preferred_element_type=F32)


def dot_t(a, b):
    return lax.dot_general(a, b, (((1,), (1,)), ((), ())), preferred_element_type=F32)


def kernel(
    rhs_h, cond_h, phase_h, prhs_ref, rate_ref, gamma_ref, vox_ref, slot_ref, wgt_ref,
    xo_h, yo_ref,
    rhs, cond, phase, pack,
    kap, fx, fy, fzp, fzm, inv, xb, hx, hy, hz, cx, cy,
    back, m1, m0, m2, r1, r0, r2, r1t, r0t, r2t, sel, wc, q_scr, vc, rec, rect,
    yb, ydn, yup, yrhs, gsurf, lsend, lrecv, ssend, srecv,
    in_sem, out_sem, send_sem, recv_sem,
):
    gx = lax.axis_index("gx")
    gy = lax.axis_index("gy")
    gz = lax.axis_index("gz")
    nx, ny = lax.axis_size("gx"), lax.axis_size("gy")
    x_dn = {"gx": lax.rem(gx + nx - 1, nx)}
    x_up = {"gx": lax.rem(gx + 1, nx)}
    y_dn = {"gy": lax.rem(gy + ny - 1, ny)}
    y_up = {"gy": lax.rem(gy + 1, ny)}
    z_other = {"gz": 1 - gz}
    z_row = 7 * (1 - gz)

    def tiles(n, z):
        at = pl.ds(128 * z, 128)
        return (
            (cond_h.at[:, :, at], cond.at[:, :, z]),
            (phase_h.at[:, :, at], phase.at[:, :, z]),
            (rhs_h.at[:, :, :, at], rhs.at[:, :, :, z]),
        )[n]

    loads = [
        [pltpu.make_async_copy(*tiles(n, z), in_sem.at[n, z]) for z in range(8)] for n in range(3)
    ]
    for load in loads:
        for copy in load:
            copy.start()

    lsend[...] = jnp.zeros((8, 128), F32)
    ssend[...] = jnp.zeros((2, 8, 128), F32)
    barrier = pltpu.get_barrier_semaphore()
    for peer in (x_dn, x_up, y_dn, y_up, z_other):
        pl.semaphore_signal(barrier, inc=1, device_id=peer, device_id_type=MESH)
    pl.semaphore_wait(barrier, 5)

    def remote(src, dst, e, n, peer):
        return pltpu.make_async_remote_copy(
            src_ref=src, dst_ref=dst, send_sem=send_sem.at[e, n], recv_sem=recv_sem.at[e, n],
            device_id=peer, device_id_type=MESH,
        )

    def halo_copies(src, e):
        return (
            remote(src.at[:, 0], hx.at[e, 1], e, 0, x_dn),
            remote(src.at[:, N - 1], hx.at[e, 0], e, 1, x_up),
            remote(src.at[:, :, 0], hy.at[e, 1], e, 2, y_dn),
            remote(src.at[:, :, N - 1], hy.at[e, 0], e, 3, y_up),
            remote(src.at[:, :, :, z_row], hz.at[e], e, 4, z_other),
        )

    def sum_copies(e):
        return (
            remote(ssend.at[0], srecv.at[e, 1], e, 5, y_dn),
            remote(ssend.at[1], srecv.at[e, 0], e, 6, y_up),
        )

    def last_copies(e):
        return (
            remote(lsend, lrecv.at[e, 1], e, 7, y_dn),
            remote(lsend, lrecv.at[e, 0], e, 8, y_up),
        )

    lane = lax.broadcasted_iota(jnp.int32, (8, 128), 1)
    sub = lax.broadcasted_iota(jnp.int32, (8, 128), 0)

    for copy in loads[0] + loads[1]:
        copy.wait()

    def kappa_plane(i, _):
        for j in range(N):
            c, p = cond[i, j], phase[i, j]
            for f in range(2):
                kap[f, i, j] = c * pick(p, conduct[f])
        return 0

    lax.fori_loop(0, N, kappa_plane, 0)
    kap_copies = halo_copies(kap, 0)
    for copy in kap_copies:
        copy.start()

    rec[...] = jnp.zeros((128, 128), F32)
    for o in range(3):
        for q in range(4):
            at = pl.ds(128 * q, 128)
            rec[pl.ds(o * 4 + q, 1), :] = vox_ref[o, :, at].astype(F32)
            rec[pl.ds(12 + o * 4 + q, 1), :] = slot_ref[o, :, at].astype(F32)
            rec[pl.ds(24 + o * 4 + q, 1), :] = wgt_ref[o, :, at]
    rect[...] = jnp.transpose(rec[...])

    for o, ref, width in ((0, r0, 512), (1, r1, 2048), (2, r2, 512)):
        for q in range(4):
            n = o * 4 + q
            voxel = rect[:, n : n + 1]
            slot = rect[:, 12 + n : 13 + n]
            weight = rect[:, 24 + n : 25 + n]
            row = jnp.floor(voxel * (1.0 / 128.0))
            at_lane = voxel - row * 128.0
            if o != 1:
                plane = jnp.floor(row * (1.0 / 128.0))
                row = row - plane * 96.0 - (96.0 if o == 2 else 0.0)
            lanes = lax.broadcasted_iota(jnp.int32, (128, 128), 1).astype(F32)
            wc[o, pl.ds(128 * q, 128), :] = jnp.where(lanes == at_lane, weight, 0.0)
            for h in range(2):
                hit = (lanes + 128.0 * h) == slot
                sel[o, pl.ds(128 * q, 128), pl.ds(128 * h, 128)] = jnp.where(hit, 1.0, 0.0).astype(BF16)
            for h in range(width // 128):
                hit = (lanes + 128.0 * h) == row
                ref[pl.ds(128 * q, 128), pl.ds(128 * h, 128)] = jnp.where(hit, 1.0, 0.0).astype(BF16)

    for o, ref, width in ((0, r0t, 512), (1, r1t, 2048), (2, r2t, 512)):
        row = lax.shift_right_logical(vox_ref[o], 7)
        if o != 1:
            row = row - lax.shift_right_logical(row, 7) * 96 - (96 if o == 2 else 0)

        def fill(c, _, ref=ref, row=row):
            at = pl.multiple_of(c * 64, 64)
            down = lax.broadcasted_iota(jnp.int32, (64, 512), 0) + at
            ref[pl.ds(at, 64), :] = jnp.where(down == row, 1.0, 0.0).astype(BF16)
            return 0

        lax.fori_loop(0, width // 64, fill, 0)

    def particle_sums(src):
        sums = []
        for o in range(3):
            both = jnp.concatenate(split(src[o]), axis=1)
            per_record = dot_t(jnp.ones((16, 256), BF16), both)
            parts = dot(jnp.concatenate(split(per_record), axis=0), sel[o])
            sums.append(parts[0:1] + parts[16:17])
        return sums

    def send_sums(sums, e):
        for d, s in ((0, sums[0]), (1, sums[2])):
            ssend[d, 0:1, :] = s[:, :128]
            ssend[d, 1:2, :] = s[:, 128:]
        for copy in sum_copies(e):
            copy.start()
        return sums[1]

    def to_voxels():
        full = dot(r1t[...], vc[1])
        back[...] = full[:, :128] + full[:, 128:]
        for o, ref, base in ((0, r0t, 0), (2, r2t, 96)):
            part = dot(ref[...], vc[o])
            part = part[:, :128] + part[:, 128:]
            for i in range(N):
                back[pl.ds(i * 128 + base, 32), :] += part[i * 32 : i * 32 + 32]

    own_weight = send_sums(particle_sums(wc), 0)
    for o in range(3):
        hi, lo = split(wc[o])
        vc[o, :, 0:128] = hi
        vc[o, :, 128:256] = lo
    to_voxels()

    kap_copies[4].wait_recv()
    first_z = (gz == 0).astype(F32)

    fx[:, 0] = jnp.zeros((2, N, 8, 128), F32)
    fx[:, N] = jnp.zeros((2, N, 8, 128), F32)

    def face_plane(i, _):
        below = jnp.maximum(i - 1, 0)
        not_first = (i > 0).astype(F32)
        for f in range(2):
            for j in range(N):
                k = kap[f, i, j]
                row = jnp.broadcast_to(hz[0, f, i, pl.ds(j, 1), :], (8, 128))
                fx[f, i, j] = not_first * face(k, kap[f, below, j])
                if j:
                    fy[f, i, j] = face(k, kap[f, i, j - 1])
                nxt = ahead(k, row * first_z, lane, sub)
                up = face(k, nxt)
                fzp[f, i, j] = up
                prev = behind(k, row * (1.0 - first_z), lane, sub)
                fzm[f, i, j] = face(k, prev)
        return 0

    lax.fori_loop(0, N, face_plane, 0)

    def diag_plane(i, _):
        for f in range(2):
            for j in range(N):
                d = pick(phase[i, j], masses[f]) + coupling[f] * back[pl.ds(pl.multiple_of(i * 128 + j * 8, 8), 8), :]
                d = d + fx[f, i, j] + fx[f, i + 1, j] + fzp[f, i, j] + fzm[f, i, j]
                if j:
                    d = d + fy[f, i, j]
                if j < N - 1:
                    d = d + fy[f, i, j + 1]
                inv[f, i, j] = d
        return 0

    lax.fori_loop(0, N, diag_plane, 0)

    for copy in kap_copies[:4]:
        copy.wait_recv()
    inside = (
        (gx > 0).astype(F32), (gx < nx - 1).astype(F32),
        (gy > 0).astype(F32), (gy < ny - 1).astype(F32),
    )

    def rim_faces(n, _):
        for f in range(2):
            for d, at in ((0, 0), (1, N - 1)):
                c = inside[d] * face(kap[f, at, n], hx[0, d, f, n])
                cx[d, f, n] = c
                inv[f, at, n] += c
            for d, at in ((0, 0), (1, N - 1)):
                c = inside[2 + d] * face(kap[f, n, at], hy[0, d, f, n])
                cy[d, f, n] = c
                inv[f, n, at] += c
        return 0

    lax.fori_loop(0, N, rim_faces, 0)
    for copy in loads[2]:
        copy.wait()

    def start_plane(i, _):
        for f in range(2):
            for j in range(N):
                v = inverse(inv[f, i, j])
                inv[f, i, j] = v
                xb[0, f, i, j] = rhs[f, i, j] * v
        return 0

    lax.fori_loop(0, N, start_plane, 0)

    def rim_scale(n, _):
        for f in range(2):
            for d, at in ((0, 0), (1, N - 1)):
                cx[d, f, n] *= inv[f, at, n]
                cy[d, f, n] *= inv[f, n, at]
        return 0

    lax.fori_loop(0, N, rim_scale, 0)

    pack[...] = jnp.zeros((128, PACKED), F32)
    rates = []
    for g, (base, rows) in enumerate(groups):
        for c in range(4):
            cls = 4 * g + c
            count = shell_counts[cls]
            start, end = shell_starts[cls], base + rows
            pack[32 * c : 32 * c + 32, end - count : end] = prhs_ref[:, start : start + count]
        rates.append(
            [
                jnp.concatenate([ref[4 * g + c : 4 * g + c + 1, :] for c in range(4)], axis=1)
                for ref in (rate_ref, gamma_ref)
            ]
        )
    for b in range(0, PACKED, 128):
        yb[b : b + 128, :] = jnp.transpose(pack[:, b : b + 128])
    for copy in sum_copies(0):
        copy.wait_recv()
    for g, (base, rows) in enumerate(groups):
        rate, gamma = rates[g]
        sums = own_weight[:, 128 * g : 128 * g + 128] + srecv[0, 0, g : g + 1, :] + srecv[0, 1, g : g + 1, :]
        down = lax.broadcasted_iota(jnp.int32, (rows, 128), 0)
        part = lax.broadcasted_iota(jnp.int32, (rows, 128), 1) // 32
        cnt = shell_counts[4 * g : 4 * g + 4]
        count = jnp.where(part == 0, cnt[0], jnp.where(part == 1, cnt[1], jnp.where(part == 2, cnt[2], cnt[3])))
        s = (down - (rows - count)).astype(F32)
        live = s >= 0.0
        last = down == rows - 1
        count = count.astype(F32)
        unit = inverse(count)
        lower = jnp.where(live, (s * unit) * (s * unit), 0.0)
        upper = jnp.where(live & ~last, ((s + 1.0) * unit) * ((s + 1.0) * unit), 0.0)
        cube = 3.0 * count * count

        def over_volume(s):
            return cube * inverse(3.0 * s * s + 3.0 * s + 1.0)

        d = 1.0 + rate * ((upper + lower) * over_volume(s))
        d = d + jnp.where(last, gamma * (coupling[0] + coupling[1]) * sums, 0.0)
        d = inverse(d)
        at = pl.ds(base, rows)
        ydn[at, :] = rate * lower * over_volume(s - 1.0) * d
        yup[at, :] = rate * upper * over_volume(s + 1.0) * d
        y = yb[at, :] * d
        yrhs[at, :] = y
        yb[at, :] = y
        gsurf[pl.ds(g, 1), :] = gamma * d[rows - 1 : rows]

    for copy in kap_copies + sum_copies(0):
        copy.wait_send()

    def iteration(t, _):
        e = t + 1
        cur = lax.rem(t, 2)
        new = 1 - cur
        x = xb.at[cur]
        xn = xb.at[new]
        halos = halo_copies(x, e)
        for copy in halos:
            copy.start()
        own_last = jnp.concatenate([yb[127:128, :], yb[383:384, :]], axis=1)
        lsend[0:1, :] = yb[127:128, :]
        lsend[1:2, :] = yb[383:384, :]
        lasts = last_copies(e)
        for copy in lasts:
            copy.start()

        def mix(i, _):
            for jp in range(N // 2):
                at = pl.ds(2 * jp, 2)
                v = coupling[0] * x[0, i, at] + coupling[1] * x[1, i, at]
                hi, lo = split(v.reshape(16, 128))
                targets = [(m1, i * 128 + jp * 16)]
                if jp < 2:
                    targets.append((m0, i * 32 + jp * 16))
                if jp >= 6:
                    targets.append((m2, i * 32 + (jp - 6) * 16))
                for ref, start in targets:
                    rows = pl.ds(pl.multiple_of(start, 16), 16)
                    ref[rows, 0:128] = hi
                    ref[rows, 128:256] = lo
            return 0

        lax.fori_loop(0, N, mix, 0)
        for o, ref, m in ((0, r0, m0), (2, r2, m2), (1, r1, m1)):
            got = dot(ref[...], m[...])
            q_scr[o] = (got[:, :128] + got[:, 128:]) * wc[o]
        own_sum = send_sums(particle_sums(q_scr), e)

        for copy in lasts:
            copy.wait_recv()
        for o in range(3):
            if o == 1:
                table = own_last
            else:
                table = jnp.concatenate([lrecv[e, o // 2, 0:1, :], lrecv[e, o // 2, 1:2, :]], axis=1)
            hi, lo = split(table)
            table = jnp.concatenate(
                [jnp.broadcast_to(hi, (128, 256)), jnp.broadcast_to(lo, (128, 256))], axis=0
            )
            got = dot_t(sel[o], table)
            hi, lo = split((got[:, :128] + got[:, 128:]) * wc[o])
            vc[o, :, 0:128] = hi
            vc[o, :, 128:256] = lo
        to_voxels()

        halos[4].wait_recv()

        def plane(i, _):
            below = jnp.maximum(i - 1, 0)
            above = jnp.minimum(i + 1, N - 1)
            done = []
            for j in range(N):
                b = back[pl.ds(pl.multiple_of(i * 128 + j * 8, 8), 8), :]
                for f in range(2):
                    v = x[f, i, j]
                    row = jnp.broadcast_to(hz[e, f, i, pl.ds(j, 1), :], (8, 128))
                    acc = rhs[f, i, j] + coupling[f] * b
                    acc += fx[f, i, j] * x[f, below, j]
                    acc += fx[f, i + 1, j] * x[f, above, j]
                    if j:
                        acc += fy[f, i, j] * x[f, i, j - 1]
                    if j < N - 1:
                        acc += fy[f, i, j + 1] * x[f, i, j + 1]
                    acc += fzp[f, i, j] * ahead(v, row, lane, sub)
                    acc += fzm[f, i, j] * behind(v, row, lane, sub)
                    done.append((f, j, acc * inv[f, i, j]))
            for f, j, v in done:
                xn[f, i, j] = v
            return 0

        lax.fori_loop(0, N, plane, 0)

        for copy in sum_copies(e):
            copy.wait_recv()
        y = yb[...]
        y = yrhs[...] + ydn[...] * pltpu.roll(y, 1, 0) + yup[...] * pltpu.roll(y, PACKED - 1, 0)
        yb[...] = y
        for g, row in ((0, 127), (1, 383)):
            sums = own_sum[:, 128 * g : 128 * g + 128] + srecv[e, 0, g : g + 1, :] + srecv[e, 1, g : g + 1, :]
            yb[row : row + 1, :] += gsurf[pl.ds(g, 1), :] * sums

        for copy in halos[:4]:
            copy.wait_recv()

        for f in range(2):
            for d, at in ((0, 0), (1, N - 1)):
                xn[f, at] += cx[d, f] * hx[e, d, f]
            for d, at in ((0, 0), (1, N - 1)):
                xn[f, :, at] += cy[d, f] * hy[e, d, f]
        for copy in halos + lasts + sum_copies(e):
            copy.wait_send()
        return 0

    lax.fori_loop(0, ITERS, iteration, 0)

    outs = [
        pltpu.make_async_copy(
            xb.at[0, :, :, :, z], xo_h.at[:, :, :, pl.ds(128 * z, 128)], out_sem.at[z]
        )
        for z in range(8)
    ]
    for copy in outs:
        copy.start()
    for b in range(0, PACKED, 128):
        pack[:, b : b + 128] = jnp.transpose(yb[b : b + 128, :])
    for g, (base, rows) in enumerate(groups):
        for c in range(4):
            cls = 4 * g + c
            count = shell_counts[cls]
            start, end = shell_starts[cls], base + rows
            yo_ref[:, start : start + count] = pack[32 * c : 32 * c + 32, end - count : end]
    for copy in outs:
        copy.wait()


def shards(
    adjoint_rhs, conductance, phase, particle_rhs, diffusion_rate, exchange_rate,
    record_voxel, record_slot, record_weight,
):
    vmem = pl.BlockSpec(memory_space=pltpu.VMEM)
    hbm = pl.BlockSpec(memory_space=pl.ANY)
    field = (2, N, N, 8, 128)
    col = (8, 128)
    scratch = [
        pltpu.VMEM(field, F32),
        pltpu.VMEM(field[1:], F32),
        pltpu.VMEM(field[1:], jnp.int32),
        pltpu.VMEM((128, PACKED), F32),
        pltpu.VMEM(field, F32),
        pltpu.VMEM((2, N + 1, N, *col), F32),
        pltpu.VMEM(field, F32),
        pltpu.VMEM(field, F32),
        pltpu.VMEM(field, F32),
        pltpu.VMEM(field, F32),
        pltpu.VMEM((2, *field), F32),
        pltpu.VMEM((5, 2, 2, N, *col), F32),
        pltpu.VMEM((5, 2, 2, N, *col), F32),
        pltpu.VMEM((5, 2, N, N, 128), F32),
        pltpu.VMEM((2, 2, N, *col), F32),
        pltpu.VMEM((2, 2, N, *col), F32),
        pltpu.VMEM((2048, 128), F32),
        pltpu.VMEM((2048, 256), BF16),
        pltpu.VMEM((512, 256), BF16),
        pltpu.VMEM((512, 256), BF16),
        pltpu.VMEM((512, 2048), BF16),
        pltpu.VMEM((512, 512), BF16),
        pltpu.VMEM((512, 512), BF16),
        pltpu.VMEM((2048, 512), BF16),
        pltpu.VMEM((512, 512), BF16),
        pltpu.VMEM((512, 512), BF16),
        pltpu.VMEM((3, 512, 256), BF16),
        pltpu.VMEM((3, 512, 128), F32),
        pltpu.VMEM((3, 512, 128), F32),
        pltpu.VMEM((3, 512, 256), BF16),
        pltpu.VMEM((128, 128), F32),
        pltpu.VMEM((128, 128), F32),
        pltpu.VMEM((PACKED, 128), F32),
        pltpu.VMEM((PACKED, 128), F32),
        pltpu.VMEM((PACKED, 128), F32),
        pltpu.VMEM((PACKED, 128), F32),
        pltpu.VMEM(col, F32),
        pltpu.VMEM(col, F32),
        pltpu.VMEM((5, 2, *col), F32),
        pltpu.VMEM((2, *col), F32),
        pltpu.VMEM((5, 2, *col), F32),
        pltpu.SemaphoreType.DMA((3, 8)),
        pltpu.SemaphoreType.DMA((8,)),
        pltpu.SemaphoreType.DMA((5, 9)),
        pltpu.SemaphoreType.DMA((5, 9)),
    ]
    x, y = pl.pallas_call(
        kernel,
        out_shape=(
            jax.ShapeDtypeStruct(adjoint_rhs.shape, F32),
            jax.ShapeDtypeStruct((32, 1200), F32),
        ),
        in_specs=[hbm, hbm, hbm, vmem, vmem, vmem, vmem, vmem, vmem],
        out_specs=(hbm, vmem),
        scratch_shapes=scratch,
        compiler_params=pltpu.CompilerParams(
            collective_id=0, has_side_effects=True, vmem_limit_bytes=56 * 1024 * 1024
        ),
    )(
        adjoint_rhs,
        conductance,
        phase,
        particle_rhs.T,
        diffusion_rate,
        exchange_rate,
        record_voxel.reshape(3, 1, 512),
        record_slot.reshape(3, 1, 512),
        record_weight.reshape(3, 1, 512),
    )
    return x, y.T


def solution(mesh):
    grid = P("gx", "gy", "gz")
    parts = P(None, ("gx", "gy", "gz"))
    return jax.shard_map(
        shards,
        mesh=mesh,
        in_specs=(P(None, "gx", "gy", "gz"), grid, grid, parts, parts, parts, grid, grid, grid),
        out_specs=(P(None, "gx", "gy", "gz"), parts),
        check_vma=False,
    )
```

```python
import jax
import jax.numpy as jnp
from jax import lax
from jax.experimental import pallas as pl
from jax.experimental.pallas import tpu as pltpu
from jax.sharding import PartitionSpec as P

ITERS = 4
shell_counts = (64, 80, 96, 128, 160, 192, 224, 256)
shell_starts = tuple(sum(shell_counts[:i]) for i in range(8))
conduct = ((1.0, 0.1, 0.5), (1.0, 0.05, 0.3))
masses = ((1.0, 0.5, 0.8), (1.0, 2.0, 1.5))
coupling = (1.0, 0.5)
groups = ((0, 128), (128, 256))
PACKED = 384

F32 = jnp.float32
BF16 = jnp.bfloat16
MESH = pl.DeviceIdType.MESH
N = 16


def pick(phase, values):
    return jnp.where(phase == 0, values[0], jnp.where(phase == 1, values[1], values[2]))


def inverse(d):
    return pl.reciprocal(d, approx=True)


def face(a, b):
    return inverse(a + b)


def split(v):
    hi = v.astype(BF16)
    lo = (v - hi.astype(F32)).astype(BF16)
    return hi, lo


def ahead(x, row, lane, sub):
    t = jnp.where(lane == 0, pltpu.roll(x, 7, 0), x)
    t = jnp.where((lane == 0) & (sub == 7), row, t)
    return pltpu.roll(t, 127, 1)


def behind(x, row, lane, sub):
    t = jnp.where(lane == 127, pltpu.roll(x, 1, 0), x)
    t = jnp.where((lane == 127) & (sub == 0), row, t)
    return pltpu.roll(t, 1, 1)


def dot(a, b):
    return jnp.dot(a, b, preferred_element_type=F32)


def dot_t(a, b):
    return lax.dot_general(a, b, (((1,), (1,)), ((), ())), preferred_element_type=F32)


def kernel(
    rhs_h, cond_h, phase_h, prhs_h, rate_h, gamma_h, vox_h, slot_h, wgt_h,
    xo_h, yo_ref,
    rhs, cond, phase, prhs_ref, rate_ref, gamma_ref, vox_ref, slot_ref, wgt_ref, pack,
    kap, fx, fy, fzp, fzm, inv, xa, xb, yface, hx, hy, hz, cx, cy,
    back, got_scr, m0, m2, r1, r0, r2, r1t, r0t, r2t, sel, wc, q_scr, vc, zface, rec, rect,
    yb, ydn, yup, yrhs, gsurf, lsend, lrecv, ssend, srecv,
    in_sem, small_sem, out_sem, send_sem, recv_sem,
):
    gx = lax.axis_index("gx")
    gy = lax.axis_index("gy")
    gz = lax.axis_index("gz")
    nx, ny = lax.axis_size("gx"), lax.axis_size("gy")
    x_dn = {"gx": lax.rem(gx + nx - 1, nx)}
    x_up = {"gx": lax.rem(gx + 1, nx)}
    y_dn = {"gy": lax.rem(gy + ny - 1, ny)}
    y_up = {"gy": lax.rem(gy + 1, ny)}
    z_other = {"gz": 1 - gz}
    z_row = 7 * (1 - gz)

    def tiles(n, z):
        at = pl.ds(128 * z, 128)
        return (
            (cond_h.at[:, :, at], cond.at[:, :, z]),
            (phase_h.at[:, :, at], phase.at[:, :, z]),
            (rhs_h.at[:, :, :, at], rhs.at[:, :, :, z]),
        )[n]

    loads = [
        [pltpu.make_async_copy(*tiles(n, z), in_sem.at[n, z]) for z in range(8)] for n in range(3)
    ]
    small = [
        pltpu.make_async_copy(src, dst, small_sem.at[n])
        for n, (src, dst) in enumerate(
            (
                (vox_h, vox_ref), (slot_h, slot_ref), (wgt_h, wgt_ref),
                (prhs_h, prhs_ref), (rate_h, rate_ref), (gamma_h, gamma_ref),
            )
        )
    ]
    for load in [small] + loads:
        for copy in load:
            copy.start()

    lsend[...] = jnp.zeros((8, 128), F32)
    ssend[...] = jnp.zeros((2, 8, 128), F32)
    barrier = pltpu.get_barrier_semaphore()
    for peer in (x_dn, x_up, y_dn, y_up, z_other):
        pl.semaphore_signal(barrier, inc=1, device_id=peer, device_id_type=MESH)

    def remote(src, dst, e, n, peer):
        return pltpu.make_async_remote_copy(
            src_ref=src, dst_ref=dst, send_sem=send_sem.at[e, n], recv_sem=recv_sem.at[e, n],
            device_id=peer, device_id_type=MESH,
        )

    def halo_copies(src, e):
        return (
            remote(src.at[:, 0], hx.at[e, 1], e, 0, x_dn),
            remote(src.at[:, N - 1], hx.at[e, 0], e, 1, x_up),
            remote(yface.at[0], hy.at[e, 1], e, 2, y_dn),
            remote(yface.at[1], hy.at[e, 0], e, 3, y_up),
            remote(src.at[:, :, :, z_row], hz.at[e], e, 4, z_other),
        )

    def start_halos(src, e):
        yface[0] = src[:, :, 0]
        yface[1] = src[:, :, N - 1]
        started = halo_copies(src, e)
        for copy in started:
            copy.start()
        return started

    def sum_copies(e):
        return (
            remote(ssend.at[0], srecv.at[e, 1], e, 5, y_dn),
            remote(ssend.at[1], srecv.at[e, 0], e, 6, y_up),
        )

    def last_copies(e):
        return (
            remote(lsend, lrecv.at[e, 1], e, 7, y_dn),
            remote(lsend, lrecv.at[e, 0], e, 8, y_up),
        )

    def start_lasts(e):
        lsend[0:1, :] = yb[127:128, :]
        lsend[1:2, :] = yb[383:384, :]
        for copy in last_copies(e):
            copy.start()

    lane = lax.broadcasted_iota(jnp.int32, (8, 128), 1)
    sub = lax.broadcasted_iota(jnp.int32, (8, 128), 0)

    for copy in small:
        copy.wait()

    rec[...] = jnp.zeros((128, 128), F32)
    for o in range(3):
        for q in range(4):
            at = pl.ds(128 * q, 128)
            rec[pl.ds(o * 4 + q, 1), :] = vox_ref[o, :, at].astype(F32)
            rec[pl.ds(12 + o * 4 + q, 1), :] = slot_ref[o, :, at].astype(F32)
            rec[pl.ds(24 + o * 4 + q, 1), :] = wgt_ref[o, :, at]
    rect[...] = jnp.transpose(rec[...])

    for o, ref, width in ((0, r0, 512), (1, r1, 2048), (2, r2, 512)):
        for q in range(4):
            n = o * 4 + q
            voxel = rect[:, n : n + 1]
            slot = rect[:, 12 + n : 13 + n]
            weight = rect[:, 24 + n : 25 + n]
            row = jnp.floor(voxel * (1.0 / 128.0))
            at_lane = voxel - row * 128.0
            if o != 1:
                plane = jnp.floor(row * (1.0 / 128.0))
                row = row - plane * 96.0 - (96.0 if o == 2 else 0.0)
            lanes = lax.broadcasted_iota(jnp.int32, (128, 128), 1).astype(F32)
            wc[o, pl.ds(128 * q, 128), :] = jnp.where(lanes == at_lane, weight, 0.0)
            for h in range(2):
                hit = (lanes + 128.0 * h) == slot
                sel[o, pl.ds(128 * q, 128), pl.ds(128 * h, 128)] = jnp.where(hit, 1.0, 0.0).astype(BF16)
            for h in range(width // 128):
                hit = (lanes + 128.0 * h) == row
                ref[pl.ds(128 * q, 128), pl.ds(128 * h, 128)] = jnp.where(hit, 1.0, 0.0).astype(BF16)

    for o, ref, width in ((0, r0t, 512), (1, r1t, 2048), (2, r2t, 512)):
        row = lax.shift_right_logical(vox_ref[o], 7)
        if o != 1:
            row = row - lax.shift_right_logical(row, 7) * 96 - (96 if o == 2 else 0)

        def fill(c, _, ref=ref, row=row):
            at = pl.multiple_of(c * 64, 64)
            down = lax.broadcasted_iota(jnp.int32, (64, 512), 0) + at
            ref[pl.ds(at, 64), :] = jnp.where(down == row, 1.0, 0.0).astype(BF16)
            return 0

        lax.fori_loop(0, width // 64, fill, 0)

    def particle_sums(src):
        sums = []
        for o in range(3):
            both = jnp.concatenate(split(src[o]), axis=1)
            per_record = dot_t(jnp.ones((16, 256), BF16), both)
            parts = dot(jnp.concatenate(split(per_record), axis=0), sel[o])
            sums.append(parts[0:1] + parts[16:17])
        return sums

    def send_sums(sums, e):
        for d, s in ((0, sums[0]), (1, sums[2])):
            ssend[d, 0:1, :] = s[:, :128]
            ssend[d, 1:2, :] = s[:, 128:]
        for copy in sum_copies(e):
            copy.start()
        return sums[1]

    def to_voxels():
        full = dot(r1t[...], vc[1])
        back[...] = full[:, :128] + full[:, 128:]
        for o, ref, base in ((0, r0t, 0), (2, r2t, 96)):
            part = dot(ref[...], vc[o])
            part = part[:, :128] + part[:, 128:]
            for i in range(N):
                back[pl.ds(i * 128 + base, 32), :] += part[i * 32 : i * 32 + 32]

    for o in range(3):
        hi, lo = split(wc[o])
        vc[o, :, 0:128] = hi
        vc[o, :, 128:256] = lo
    to_voxels()

    for copy in loads[0] + loads[1]:
        copy.wait()

    def kappa_plane(i, _):
        for j in range(N):
            c, p = cond[i, j], phase[i, j]
            r = inverse(c)
            for f in range(2):
                kap[f, i, j] = r * pick(p, [0.5 / v for v in conduct[f]])
        return 0

    lax.fori_loop(0, N, kappa_plane, 0)
    pl.semaphore_wait(barrier, 5)
    kap_copies = start_halos(kap, 0)
    own_weight = send_sums(particle_sums(wc), 0)

    kap_copies[4].wait_recv()
    first_z = (gz == 0).astype(F32)
    end_mask = jnp.where((lane == 127) & (sub == 7), first_z, 1.0)

    fx[:, 0] = jnp.zeros((2, N, 8, 128), F32)
    for f in range(2):
        for i in range(N):
            start = face(kap[f, i, :, 0, :], pltpu.roll(hz[0, f, i], 1, 1))
            zface[f, i] = pltpu.roll(start, 127, 1) * (1.0 - first_z)

    def face_plane(i, _):
        below = jnp.maximum(i - 1, 0)
        above = jnp.minimum(i + 1, N - 1)
        not_first = (i > 0).astype(F32)
        not_last = (i < N - 1).astype(F32)
        for j in range(N):
            p = phase[i, j]
            weight = back[pl.ds(pl.multiple_of(i * 128 + j * 8, 8), 8), :]
            for f in range(2):
                row = jnp.broadcast_to(hz[0, f, i, pl.ds(j, 1), :], (8, 128))
                start = jnp.broadcast_to(zface[f, i, pl.ds(j, 1), :], (8, 128))
                k = kap[f, i, j]
                d = pick(p, masses[f]) + coupling[f] * weight
                upper = not_last * face(k, kap[f, above, j])
                fx[f, i + 1, j] = upper
                d += upper + not_first * face(k, kap[f, below, j])
                if j:
                    d += face(k, kap[f, i, j - 1])
                if j < N - 1:
                    side = face(k, kap[f, i, j + 1])
                    fy[f, i, j + 1] = side
                    d += side
                up = face(k, ahead(k, row, lane, sub)) * end_mask
                down = behind(up, start, lane, sub)
                fzp[f, i, j] = up
                fzm[f, i, j] = down
                inv[f, i, j] = d + up + down
        return 0

    lax.fori_loop(0, N, face_plane, 0)

    for copy in kap_copies[:4]:
        copy.wait_recv()
    inside = (
        (gx > 0).astype(F32), (gx < nx - 1).astype(F32),
        (gy > 0).astype(F32), (gy < ny - 1).astype(F32),
    )

    def rim_faces(n, _):
        for f in range(2):
            for d, at in ((0, 0), (1, N - 1)):
                c = inside[d] * face(kap[f, at, n], hx[0, d, f, n])
                cx[d, f, n] = c
                inv[f, at, n] += c
            for d, at in ((0, 0), (1, N - 1)):
                c = inside[2 + d] * face(kap[f, n, at], hy[0, d, f, n])
                cy[d, f, n] = c
                inv[f, n, at] += c
        return 0

    lax.fori_loop(0, N, rim_faces, 0)
    for copy in loads[2]:
        copy.wait()

    def start_plane(i, _):
        for f in range(2):
            for j in range(N):
                v = inverse(inv[f, i, j])
                inv[f, i, j] = v
                xa[f, i, j] = rhs[f, i, j] * v
        return 0

    lax.fori_loop(0, N, start_plane, 0)
    for copy in kap_copies:
        copy.wait_send()
    start_halos(xa, 1)

    def rim_scale(n, _):
        for f in range(2):
            for d, at in ((0, 0), (1, N - 1)):
                cx[d, f, n] *= inv[f, at, n]
                cy[d, f, n] *= inv[f, n, at]
        return 0

    lax.fori_loop(0, N, rim_scale, 0)

    pack[...] = jnp.zeros((128, PACKED), F32)
    rates = []
    for g, (base, rows) in enumerate(groups):
        for c in range(4):
            cls = 4 * g + c
            count = shell_counts[cls]
            start, end = shell_starts[cls], base + rows
            pack[32 * c : 32 * c + 32, end - count : end] = prhs_ref[:, start : start + count]
        rates.append(
            [
                jnp.concatenate([ref[4 * g + c : 4 * g + c + 1, :] for c in range(4)], axis=1)
                for ref in (rate_ref, gamma_ref)
            ]
        )
    for b in range(0, PACKED, 128):
        yb[b : b + 128, :] = jnp.transpose(pack[:, b : b + 128])
    for copy in sum_copies(0):
        copy.wait_recv()
    for g, (base, rows) in enumerate(groups):
        rate, gamma = rates[g]
        sums = own_weight[:, 128 * g : 128 * g + 128] + srecv[0, 0, g : g + 1, :] + srecv[0, 1, g : g + 1, :]
        down = lax.broadcasted_iota(jnp.int32, (rows, 128), 0)
        part = lax.broadcasted_iota(jnp.int32, (rows, 128), 1) // 32
        cnt = shell_counts[4 * g : 4 * g + 4]
        count = jnp.where(part == 0, cnt[0], jnp.where(part == 1, cnt[1], jnp.where(part == 2, cnt[2], cnt[3])))
        s = (down - (rows - count)).astype(F32)
        live = s >= 0.0
        last = down == rows - 1
        count = count.astype(F32)
        unit = inverse(count)
        lower = jnp.where(live, (s * unit) * (s * unit), 0.0)
        upper = jnp.where(live & ~last, ((s + 1.0) * unit) * ((s + 1.0) * unit), 0.0)
        cube = 3.0 * count * count

        def over_volume(s):
            return cube * inverse(3.0 * s * s + 3.0 * s + 1.0)

        d = 1.0 + rate * ((upper + lower) * over_volume(s))
        d = d + jnp.where(last, gamma * (coupling[0] + coupling[1]) * sums, 0.0)
        d = inverse(d)
        at = pl.ds(base, rows)
        ydn[at, :] = rate * lower * over_volume(s - 1.0) * d
        yup[at, :] = rate * upper * over_volume(s + 1.0) * d
        y = yb[at, :] * d
        yrhs[at, :] = y
        yb[at, :] = y
        gsurf[pl.ds(g, 1), :] = gamma * d[rows - 1 : rows]

    for copy in sum_copies(0):
        copy.wait_send()
    start_lasts(1)

    def iteration(t, x, xn):
        e = t + 1
        own_last = jnp.concatenate([yb[127:128, :], yb[383:384, :]], axis=1)
        lasts = last_copies(e)
        halos = halo_copies(x, e)

        got_scr[...] = jnp.zeros((512, 256), F32)
        halos[4].wait_recv()

        def planes(s, _):
            mixed = []
            for h in range(2):
                i = 2 * s + h
                below = jnp.maximum(i - 1, 0)
                above = jnp.minimum(i + 1, N - 1)
                for j in range(N):
                    mixed.append(coupling[0] * x[0, i, j] + coupling[1] * x[1, i, j])
                    for f in range(2):
                        v = x[f, i, j]
                        row = jnp.broadcast_to(hz[e, f, i, pl.ds(j, 1), :], (8, 128))
                        acc = rhs[f, i, j]
                        acc += fx[f, i, j] * x[f, below, j]
                        acc += fx[f, i + 1, j] * x[f, above, j]
                        if j:
                            acc += fy[f, i, j] * x[f, i, j - 1]
                        if j < N - 1:
                            acc += fy[f, i, j + 1] * x[f, i, j + 1]
                        acc += fzp[f, i, j] * ahead(v, row, lane, sub)
                        acc += fzm[f, i, j] * behind(v, row, lane, sub)
                        xn[f, i, j] = acc * inv[f, i, j]
            parts = []
            for n in range(0, 2 * N, 2):
                h, j = divmod(n, N)
                part = jnp.concatenate(split(jnp.concatenate(mixed[n : n + 2], axis=0)), axis=1)
                parts.append(part)
                for ref, first in ((m0, 0), (m2, 12)):
                    if first <= j < first + 4:
                        at = (2 * s + h) * 32 + (j - first) * 8
                        ref[pl.ds(pl.multiple_of(at, 16), 16), :] = part
            at = pl.ds(pl.multiple_of(s * 256, 256), 256)
            got_scr[...] += dot(r1[:, at], jnp.concatenate(parts, axis=0))
            return 0

        lax.fori_loop(0, N // 2, planes, 0)

        for o, ref, m in ((0, r0, m0), (2, r2, m2), (1, None, None)):
            got = got_scr[...] if o == 1 else dot(ref[...], m[...])
            q_scr[o] = (got[:, :128] + got[:, 128:]) * wc[o]
        own_sum = send_sums(particle_sums(q_scr), e)

        for copy in lasts:
            copy.wait_recv()
        for o in range(3):
            if o == 1:
                table = own_last
            else:
                table = jnp.concatenate([lrecv[e, o // 2, 0:1, :], lrecv[e, o // 2, 1:2, :]], axis=1)
            hi, lo = split(table)
            table = jnp.concatenate(
                [jnp.broadcast_to(hi, (128, 256)), jnp.broadcast_to(lo, (128, 256))], axis=0
            )
            got = dot_t(sel[o], table)
            hi, lo = split((got[:, :128] + got[:, 128:]) * wc[o])
            vc[o, :, 0:128] = hi
            vc[o, :, 128:256] = lo
        to_voxels()

        def records(i, _):
            rows = pl.ds(pl.multiple_of(i * 128, 128), 128)
            b = back[rows, :].reshape(N, 8, 128)
            sums = [xn[f, i] + coupling[f] * b * inv[f, i] for f in range(2)]
            for f in range(2):
                xn[f, i] = sums[f]
            return 0

        lax.fori_loop(0, N, records, 0)
        for copy in halos[:4]:
            copy.wait_recv()
        for f in range(2):
            for d, at in ((0, 0), (1, N - 1)):
                xn[f, at] += cx[d, f] * hx[e, d, f]
            for d, at in ((0, 0), (1, N - 1)):
                xn[f, :, at] += cy[d, f] * hy[e, d, f]
        for copy in halos:
            copy.wait_send()

        @pl.when(t < ITERS - 1)
        def _():
            start_halos(xn, e + 1)

        for copy in sum_copies(e):
            copy.wait_recv()
        y = yb[...]
        y = yrhs[...] + ydn[...] * pltpu.roll(y, 1, 0) + yup[...] * pltpu.roll(y, PACKED - 1, 0)
        yb[...] = y
        for g, row in ((0, 127), (1, 383)):
            sums = own_sum[:, 128 * g : 128 * g + 128] + srecv[e, 0, g : g + 1, :] + srecv[e, 1, g : g + 1, :]
            yb[row : row + 1, :] += gsurf[pl.ds(g, 1), :] * sums
        for copy in lasts + sum_copies(e):
            copy.wait_send()

        @pl.when(t < ITERS - 1)
        def _():
            start_lasts(e + 1)

    def two_iterations(u, _):
        iteration(2 * u, xa, xb)
        iteration(2 * u + 1, xb, xa)
        return 0

    lax.fori_loop(0, ITERS // 2, two_iterations, 0)

    outs = [
        pltpu.make_async_copy(
            xa.at[:, :, :, z], xo_h.at[:, :, :, pl.ds(128 * z, 128)], out_sem.at[z]
        )
        for z in range(8)
    ]
    for copy in outs:
        copy.start()
    for b in range(0, PACKED, 128):
        pack[:, b : b + 128] = jnp.transpose(yb[b : b + 128, :])
    for g, (base, rows) in enumerate(groups):
        for c in range(4):
            cls = 4 * g + c
            count = shell_counts[cls]
            start, end = shell_starts[cls], base + rows
            yo_ref[:, start : start + count] = pack[32 * c : 32 * c + 32, end - count : end]
    for copy in outs:
        copy.wait()


def shards(
    adjoint_rhs, conductance, phase, particle_rhs, diffusion_rate, exchange_rate,
    record_voxel, record_slot, record_weight,
):
    vmem = pl.BlockSpec(memory_space=pltpu.VMEM)
    hbm = pl.BlockSpec(memory_space=pltpu.HBM)
    free = pl.BlockSpec(memory_space=pl.ANY)
    field = (2, N, N, 8, 128)
    col = (8, 128)
    scratch = [
        pltpu.VMEM(field, F32),
        pltpu.VMEM(field[1:], F32),
        pltpu.VMEM(field[1:], jnp.int32),
        pltpu.VMEM((32, 1200), F32),
        pltpu.VMEM((8, 32), F32),
        pltpu.VMEM((8, 32), F32),
        pltpu.VMEM((3, 1, 512), jnp.int32),
        pltpu.VMEM((3, 1, 512), jnp.int32),
        pltpu.VMEM((3, 1, 512), F32),
        pltpu.VMEM((128, PACKED), F32),
        pltpu.VMEM(field, F32),
        pltpu.VMEM((2, N + 1, N, *col), F32),
        pltpu.VMEM(field, F32),
        pltpu.VMEM(field, F32),
        pltpu.VMEM(field, F32),
        pltpu.VMEM(field, F32),
        pltpu.VMEM(field, F32),
        pltpu.VMEM(field, F32),
        pltpu.VMEM((2, 2, N, *col), F32),
        pltpu.VMEM((5, 2, 2, N, *col), F32),
        pltpu.VMEM((5, 2, 2, N, *col), F32),
        pltpu.VMEM((5, 2, N, N, 128), F32),
        pltpu.VMEM((2, 2, N, *col), F32),
        pltpu.VMEM((2, 2, N, *col), F32),
        pltpu.VMEM((2048, 128), F32),
        pltpu.VMEM((512, 256), F32),
        pltpu.VMEM((512, 256), BF16),
        pltpu.VMEM((512, 256), BF16),
        pltpu.VMEM((512, 2048), BF16),
        pltpu.VMEM((512, 512), BF16),
        pltpu.VMEM((512, 512), BF16),
        pltpu.VMEM((2048, 512), BF16),
        pltpu.VMEM((512, 512), BF16),
        pltpu.VMEM((512, 512), BF16),
        pltpu.VMEM((3, 512, 256), BF16),
        pltpu.VMEM((3, 512, 128), F32),
        pltpu.VMEM((3, 512, 128), F32),
        pltpu.VMEM((3, 512, 256), BF16),
        pltpu.VMEM((2, N, N, 128), F32),
        pltpu.VMEM((128, 128), F32),
        pltpu.VMEM((128, 128), F32),
        pltpu.VMEM((PACKED, 128), F32),
        pltpu.VMEM((PACKED, 128), F32),
        pltpu.VMEM((PACKED, 128), F32),
        pltpu.VMEM((PACKED, 128), F32),
        pltpu.VMEM(col, F32),
        pltpu.VMEM(col, F32),
        pltpu.VMEM((5, 2, *col), F32),
        pltpu.VMEM((2, *col), F32),
        pltpu.VMEM((5, 2, *col), F32),
        pltpu.SemaphoreType.DMA((3, 8)),
        pltpu.SemaphoreType.DMA((6,)),
        pltpu.SemaphoreType.DMA((8,)),
        pltpu.SemaphoreType.DMA((5, 9)),
        pltpu.SemaphoreType.DMA((5, 9)),
    ]
    x, y = pl.pallas_call(
        kernel,
        out_shape=(
            jax.ShapeDtypeStruct(adjoint_rhs.shape, F32),
            jax.ShapeDtypeStruct((32, 1200), F32),
        ),
        in_specs=[hbm] * 9,
        out_specs=(free, vmem),
        scratch_shapes=scratch,
        compiler_params=pltpu.CompilerParams(
            collective_id=0, has_side_effects=True, vmem_limit_bytes=56 * 1024 * 1024
        ),
    )(
        adjoint_rhs,
        conductance,
        phase,
        particle_rhs.T,
        diffusion_rate,
        exchange_rate,
        record_voxel.reshape(3, 1, 512),
        record_slot.reshape(3, 1, 512),
        record_weight.reshape(3, 1, 512),
    )
    return x, y.T


def solution(mesh):
    grid = P("gx", "gy", "gz")
    parts = P(None, ("gx", "gy", "gz"))
    return jax.shard_map(
        shards,
        mesh=mesh,
        in_specs=(P(None, "gx", "gy", "gz"), grid, grid, parts, parts, parts, grid, grid, grid),
        out_specs=(P(None, "gx", "gy", "gz"), parts),
        check_vma=False,
    )
```

```python
import jax
import jax.numpy as jnp
from jax import lax
from jax.experimental import pallas as pl
from jax.experimental.pallas import tpu as pltpu
from jax.sharding import PartitionSpec as P

ITERS = 4
shell_counts = (64, 80, 96, 128, 160, 192, 224, 256)
shell_starts = tuple(sum(shell_counts[:i]) for i in range(8))
conduct = ((1.0, 0.1, 0.5), (1.0, 0.05, 0.3))
masses = ((1.0, 0.5, 0.8), (1.0, 2.0, 1.5))
coupling = (1.0, 0.5)
groups = ((0, 128), (128, 256))
PACKED = 384

F32 = jnp.float32
BF16 = jnp.bfloat16
MESH = pl.DeviceIdType.MESH
N = 16


def pick(phase, values):
    return jnp.where(phase == 0, values[0], jnp.where(phase == 1, values[1], values[2]))


def inverse(d):
    return pl.reciprocal(d, approx=True)


def face(a, b):
    return inverse(a + b)


def split(v):
    hi = v.astype(BF16)
    lo = (v - hi.astype(F32)).astype(BF16)
    return hi, lo


def ahead(x, row, lane, sub):
    t = jnp.where(lane == 0, pltpu.roll(x, 7, 0), x)
    t = jnp.where((lane == 0) & (sub == 7), row, t)
    return pltpu.roll(t, 127, 1)


def behind(x, row, lane, sub):
    t = jnp.where(lane == 127, pltpu.roll(x, 1, 0), x)
    t = jnp.where((lane == 127) & (sub == 0), row, t)
    return pltpu.roll(t, 1, 1)


def dot(a, b):
    return jnp.dot(a, b, preferred_element_type=F32)


def dot_t(a, b):
    return lax.dot_general(a, b, (((1,), (1,)), ((), ())), preferred_element_type=F32)


class Guarded:
    def __init__(self, copy, sends, receives):
        self.copy, self.sends, self.receives = copy, sends, receives

    def start(self):
        pl.when(self.sends)(self.copy.start)

    def wait_send(self):
        pl.when(self.sends)(self.copy.wait_send)

    def wait_recv(self):
        pl.when(self.receives)(self.copy.wait_recv)


def kernel(
    rhs_h, cond_h, phase_h, prhs_h, rate_h, gamma_h, vox_h, slot_h, wgt_h,
    xo_h, yo_ref,
    rhs, cond, phase, prhs_ref, rate_ref, gamma_ref, vox_ref, slot_ref, wgt_ref, pack,
    kap, fx, fy, fzp, fzm, inv, xa, xb, yface, hx, hy, hz, cx, cy,
    back, got_scr, m0, m2, r1, r0, r2, r1t, r0t, r2t, sel, wc, q_scr, vc, zface, rec, rect,
    yb, ydn, yup, yrhs, gsurf, lsend, lrecv, ssend, srecv,
    in_sem, small_sem, out_sem, send_sem, recv_sem,
):
    gx = lax.axis_index("gx")
    gy = lax.axis_index("gy")
    gz = lax.axis_index("gz")
    nx, ny = lax.axis_size("gx"), lax.axis_size("gy")
    x_dn = {"gx": lax.rem(gx + nx - 1, nx)}
    x_up = {"gx": lax.rem(gx + 1, nx)}
    y_dn = {"gy": lax.rem(gy + ny - 1, ny)}
    y_up = {"gy": lax.rem(gy + 1, ny)}
    z_other = {"gz": 1 - gz}
    z_row = 7 * (1 - gz)

    def tiles(n, z):
        at = pl.ds(128 * z, 128)
        return (
            (cond_h.at[:, :, at], cond.at[:, :, z]),
            (phase_h.at[:, :, at], phase.at[:, :, z]),
            (rhs_h.at[:, :, :, at], rhs.at[:, :, :, z]),
        )[n]

    loads = [
        [pltpu.make_async_copy(*tiles(n, z), in_sem.at[n, z]) for z in range(8)] for n in range(3)
    ]
    small = [
        pltpu.make_async_copy(src, dst, small_sem.at[n])
        for n, (src, dst) in enumerate(
            (
                (vox_h, vox_ref), (slot_h, slot_ref), (wgt_h, wgt_ref),
                (prhs_h, prhs_ref), (rate_h, rate_ref), (gamma_h, gamma_ref),
            )
        )
    ]
    for load in [small] + loads:
        for copy in load:
            copy.start()

    has_x_dn, has_x_up = gx > 0, gx < nx - 1
    has_y_dn, has_y_up = gy > 0, gy < ny - 1
    ways = {}
    for n in (0, 2, 5, 7):
        dn, up = (has_x_dn, has_x_up) if n == 0 else (has_y_dn, has_y_up)
        ways[n], ways[n + 1] = (dn, up), (up, dn)

    for missing, ref, d in (
        (gx == 0, hx, 0), (gx == nx - 1, hx, 1), (gy == 0, hy, 0), (gy == ny - 1, hy, 1)
    ):

        @pl.when(missing)
        def _(ref=ref, d=d):
            ref[:, d] = jnp.zeros((5, 2, N, 8, 128), F32)

    lrecv[...] = jnp.zeros((5, 2, 8, 128), F32)
    srecv[...] = jnp.zeros((5, 2, 8, 128), F32)
    lsend[...] = jnp.zeros((8, 128), F32)
    ssend[...] = jnp.zeros((2, 8, 128), F32)
    barrier = pltpu.get_barrier_semaphore()
    greeted = jnp.int32(1)
    pl.semaphore_signal(barrier, inc=1, device_id=z_other, device_id_type=MESH)
    for there, peer in ((has_x_dn, x_dn), (has_x_up, x_up), (has_y_dn, y_dn), (has_y_up, y_up)):
        greeted += there.astype(jnp.int32)

        @pl.when(there)
        def _(peer=peer):
            pl.semaphore_signal(barrier, inc=1, device_id=peer, device_id_type=MESH)


    def remote(src, dst, e, n, peer):
        copy = pltpu.make_async_remote_copy(
            src_ref=src, dst_ref=dst, send_sem=send_sem.at[e, n], recv_sem=recv_sem.at[e, n],
            device_id=peer, device_id_type=MESH,
        )
        if n == 4:
            return copy
        sends, receives = ways[n]
        return Guarded(copy, sends, receives)

    def halo_copies(src, e):
        return (
            remote(src.at[:, 0], hx.at[e, 1], e, 0, x_dn),
            remote(src.at[:, N - 1], hx.at[e, 0], e, 1, x_up),
            remote(yface.at[0], hy.at[e, 1], e, 2, y_dn),
            remote(yface.at[1], hy.at[e, 0], e, 3, y_up),
            remote(src.at[:, :, :, z_row], hz.at[e], e, 4, z_other),
        )

    def start_halos(src, e):
        yface[0] = src[:, :, 0]
        yface[1] = src[:, :, N - 1]
        started = halo_copies(src, e)
        for copy in started:
            copy.start()
        return started

    def sum_copies(e):
        return (
            remote(ssend.at[0], srecv.at[e, 1], e, 5, y_dn),
            remote(ssend.at[1], srecv.at[e, 0], e, 6, y_up),
        )

    def last_copies(e):
        return (
            remote(lsend, lrecv.at[e, 1], e, 7, y_dn),
            remote(lsend, lrecv.at[e, 0], e, 8, y_up),
        )

    def start_lasts(e):
        lsend[0:1, :] = yb[127:128, :]
        lsend[1:2, :] = yb[383:384, :]
        for copy in last_copies(e):
            copy.start()

    lane = lax.broadcasted_iota(jnp.int32, (8, 128), 1)
    sub = lax.broadcasted_iota(jnp.int32, (8, 128), 0)

    for copy in small:
        copy.wait()

    rec[...] = jnp.zeros((128, 128), F32)
    for o in range(3):
        for q in range(4):
            at = pl.ds(128 * q, 128)
            rec[pl.ds(o * 4 + q, 1), :] = vox_ref[o, :, at].astype(F32)
            rec[pl.ds(12 + o * 4 + q, 1), :] = slot_ref[o, :, at].astype(F32)
            rec[pl.ds(24 + o * 4 + q, 1), :] = wgt_ref[o, :, at]
    rect[...] = jnp.transpose(rec[...])

    for o, ref, width in ((0, r0, 512), (1, r1, 2048), (2, r2, 512)):
        for q in range(4):
            n = o * 4 + q
            voxel = rect[:, n : n + 1]
            slot = rect[:, 12 + n : 13 + n]
            weight = rect[:, 24 + n : 25 + n]
            row = jnp.floor(voxel * (1.0 / 128.0))
            at_lane = voxel - row * 128.0
            if o != 1:
                plane = jnp.floor(row * (1.0 / 128.0))
                row = row - plane * 96.0 - (96.0 if o == 2 else 0.0)
            lanes = lax.broadcasted_iota(jnp.int32, (128, 128), 1).astype(F32)
            wc[o, pl.ds(128 * q, 128), :] = jnp.where(lanes == at_lane, weight, 0.0)
            for h in range(2):
                hit = (lanes + 128.0 * h) == slot
                sel[o, pl.ds(128 * q, 128), pl.ds(128 * h, 128)] = jnp.where(hit, 1.0, 0.0).astype(BF16)
            for h in range(width // 128):
                hit = (lanes + 128.0 * h) == row
                ref[pl.ds(128 * q, 128), pl.ds(128 * h, 128)] = jnp.where(hit, 1.0, 0.0).astype(BF16)

    for o, ref, width in ((0, r0t, 512), (1, r1t, 2048), (2, r2t, 512)):
        row = lax.shift_right_logical(vox_ref[o], 7)
        if o != 1:
            row = row - lax.shift_right_logical(row, 7) * 96 - (96 if o == 2 else 0)

        def fill(c, _, ref=ref, row=row):
            at = pl.multiple_of(c * 64, 64)
            down = lax.broadcasted_iota(jnp.int32, (64, 512), 0) + at
            ref[pl.ds(at, 64), :] = jnp.where(down == row, 1.0, 0.0).astype(BF16)
            return 0

        lax.fori_loop(0, width // 64, fill, 0)

    def particle_sums(src):
        sums = []
        for o in range(3):
            both = jnp.concatenate(split(src[o]), axis=1)
            per_record = dot_t(jnp.ones((16, 256), BF16), both)
            parts = dot(jnp.concatenate(split(per_record), axis=0), sel[o])
            sums.append(parts[0:1] + parts[16:17])
        return sums

    def send_sums(sums, e):
        for d, s in ((0, sums[0]), (1, sums[2])):
            ssend[d, 0:1, :] = s[:, :128]
            ssend[d, 1:2, :] = s[:, 128:]
        for copy in sum_copies(e):
            copy.start()
        return sums[1]

    def to_voxels():
        full = dot(r1t[...], vc[1])
        back[...] = full[:, :128] + full[:, 128:]
        for o, ref, base in ((0, r0t, 0), (2, r2t, 96)):
            part = dot(ref[...], vc[o])
            part = part[:, :128] + part[:, 128:]
            for i in range(N):
                back[pl.ds(i * 128 + base, 32), :] += part[i * 32 : i * 32 + 32]

    for o in range(3):
        hi, lo = split(wc[o])
        vc[o, :, 0:128] = hi
        vc[o, :, 128:256] = lo
    to_voxels()

    for copy in loads[0] + loads[1]:
        copy.wait()

    def kappa_plane(i, _):
        for j in range(N):
            c, p = cond[i, j], phase[i, j]
            r = inverse(c)
            for f in range(2):
                kap[f, i, j] = r * pick(p, [0.5 / v for v in conduct[f]])
        return 0

    lax.fori_loop(0, N, kappa_plane, 0)
    pl.semaphore_wait(barrier, greeted)
    kap_copies = start_halos(kap, 0)
    own_weight = send_sums(particle_sums(wc), 0)

    kap_copies[4].wait_recv()
    first_z = (gz == 0).astype(F32)
    end_mask = jnp.where((lane == 127) & (sub == 7), first_z, 1.0)

    fx[:, 0] = jnp.zeros((2, N, 8, 128), F32)
    for f in range(2):
        for i in range(N):
            start = face(kap[f, i, :, 0, :], pltpu.roll(hz[0, f, i], 1, 1))
            zface[f, i] = pltpu.roll(start, 127, 1) * (1.0 - first_z)

    def face_plane(i, _):
        below = jnp.maximum(i - 1, 0)
        above = jnp.minimum(i + 1, N - 1)
        not_first = (i > 0).astype(F32)
        not_last = (i < N - 1).astype(F32)
        for j in range(N):
            p = phase[i, j]
            weight = back[pl.ds(pl.multiple_of(i * 128 + j * 8, 8), 8), :]
            for f in range(2):
                row = jnp.broadcast_to(hz[0, f, i, pl.ds(j, 1), :], (8, 128))
                start = jnp.broadcast_to(zface[f, i, pl.ds(j, 1), :], (8, 128))
                k = kap[f, i, j]
                d = pick(p, masses[f]) + coupling[f] * weight
                upper = not_last * face(k, kap[f, above, j])
                fx[f, i + 1, j] = upper
                d += upper + not_first * face(k, kap[f, below, j])
                if j:
                    d += face(k, kap[f, i, j - 1])
                if j < N - 1:
                    side = face(k, kap[f, i, j + 1])
                    fy[f, i, j + 1] = side
                    d += side
                up = face(k, ahead(k, row, lane, sub)) * end_mask
                down = behind(up, start, lane, sub)
                fzp[f, i, j] = up
                fzm[f, i, j] = down
                inv[f, i, j] = d + up + down
        return 0

    lax.fori_loop(0, N, face_plane, 0)

    for copy in kap_copies[:4]:
        copy.wait_recv()
    inside = (
        (gx > 0).astype(F32), (gx < nx - 1).astype(F32),
        (gy > 0).astype(F32), (gy < ny - 1).astype(F32),
    )

    def rim_faces(n, _):
        for f in range(2):
            for d, at in ((0, 0), (1, N - 1)):
                c = inside[d] * face(kap[f, at, n], hx[0, d, f, n])
                cx[d, f, n] = c
                inv[f, at, n] += c
            for d, at in ((0, 0), (1, N - 1)):
                c = inside[2 + d] * face(kap[f, n, at], hy[0, d, f, n])
                cy[d, f, n] = c
                inv[f, n, at] += c
        return 0

    lax.fori_loop(0, N, rim_faces, 0)
    for copy in loads[2]:
        copy.wait()

    def start_plane(i, _):
        for f in range(2):
            for j in range(N):
                v = inverse(inv[f, i, j])
                inv[f, i, j] = v
                xa[f, i, j] = rhs[f, i, j] * v
        return 0

    lax.fori_loop(0, N, start_plane, 0)
    for copy in kap_copies:
        copy.wait_send()
    start_halos(xa, 1)

    def rim_scale(n, _):
        for f in range(2):
            for d, at in ((0, 0), (1, N - 1)):
                cx[d, f, n] *= inv[f, at, n]
                cy[d, f, n] *= inv[f, n, at]
        return 0

    lax.fori_loop(0, N, rim_scale, 0)

    pack[...] = jnp.zeros((128, PACKED), F32)
    rates = []
    for g, (base, rows) in enumerate(groups):
        for c in range(4):
            cls = 4 * g + c
            count = shell_counts[cls]
            start, end = shell_starts[cls], base + rows
            pack[32 * c : 32 * c + 32, end - count : end] = prhs_ref[:, start : start + count]
        rates.append(
            [
                jnp.concatenate([ref[4 * g + c : 4 * g + c + 1, :] for c in range(4)], axis=1)
                for ref in (rate_ref, gamma_ref)
            ]
        )
    for b in range(0, PACKED, 128):
        yb[b : b + 128, :] = jnp.transpose(pack[:, b : b + 128])
    for copy in sum_copies(0):
        copy.wait_recv()
    for g, (base, rows) in enumerate(groups):
        rate, gamma = rates[g]
        sums = own_weight[:, 128 * g : 128 * g + 128] + srecv[0, 0, g : g + 1, :] + srecv[0, 1, g : g + 1, :]
        down = lax.broadcasted_iota(jnp.int32, (rows, 128), 0)
        part = lax.broadcasted_iota(jnp.int32, (rows, 128), 1) // 32
        cnt = shell_counts[4 * g : 4 * g + 4]
        count = jnp.where(part == 0, cnt[0], jnp.where(part == 1, cnt[1], jnp.where(part == 2, cnt[2], cnt[3])))
        s = (down - (rows - count)).astype(F32)
        live = s >= 0.0
        last = down == rows - 1
        count = count.astype(F32)
        unit = inverse(count)
        lower = jnp.where(live, (s * unit) * (s * unit), 0.0)
        upper = jnp.where(live & ~last, ((s + 1.0) * unit) * ((s + 1.0) * unit), 0.0)
        cube = 3.0 * count * count

        def over_volume(s):
            return cube * inverse(3.0 * s * s + 3.0 * s + 1.0)

        d = 1.0 + rate * ((upper + lower) * over_volume(s))
        d = d + jnp.where(last, gamma * (coupling[0] + coupling[1]) * sums, 0.0)
        d = inverse(d)
        at = pl.ds(base, rows)
        ydn[at, :] = rate * lower * over_volume(s - 1.0) * d
        yup[at, :] = rate * upper * over_volume(s + 1.0) * d
        y = yb[at, :] * d
        yrhs[at, :] = y
        yb[at, :] = y
        gsurf[pl.ds(g, 1), :] = gamma * d[rows - 1 : rows]

    for copy in sum_copies(0):
        copy.wait_send()
    start_lasts(1)

    outs = [
        pltpu.make_async_copy(
            xa.at[:, :, :, z], xo_h.at[:, :, :, pl.ds(128 * z, 128)], out_sem.at[z]
        )
        for z in range(8)
    ]

    def iteration(t, x, xn):
        e = t + 1
        own_last = jnp.concatenate([yb[127:128, :], yb[383:384, :]], axis=1)
        lasts = last_copies(e)
        halos = halo_copies(x, e)

        got_scr[...] = jnp.zeros((512, 256), F32)
        halos[4].wait_recv()

        def planes(s, _):
            mixed = []
            for h in range(2):
                i = 2 * s + h
                below = jnp.maximum(i - 1, 0)
                above = jnp.minimum(i + 1, N - 1)
                for j in range(N):
                    mixed.append(coupling[0] * x[0, i, j] + coupling[1] * x[1, i, j])
                    for f in range(2):
                        v = x[f, i, j]
                        row = jnp.broadcast_to(hz[e, f, i, pl.ds(j, 1), :], (8, 128))
                        acc = rhs[f, i, j]
                        acc += fx[f, i, j] * x[f, below, j]
                        acc += fx[f, i + 1, j] * x[f, above, j]
                        if j:
                            acc += fy[f, i, j] * x[f, i, j - 1]
                        if j < N - 1:
                            acc += fy[f, i, j + 1] * x[f, i, j + 1]
                        acc += fzp[f, i, j] * ahead(v, row, lane, sub)
                        acc += fzm[f, i, j] * behind(v, row, lane, sub)
                        xn[f, i, j] = acc * inv[f, i, j]
            parts = []
            for n in range(0, 2 * N, 2):
                h, j = divmod(n, N)
                part = jnp.concatenate(split(jnp.concatenate(mixed[n : n + 2], axis=0)), axis=1)
                parts.append(part)
                for ref, first in ((m0, 0), (m2, 12)):
                    if first <= j < first + 4:
                        at = (2 * s + h) * 32 + (j - first) * 8
                        ref[pl.ds(pl.multiple_of(at, 16), 16), :] = part
            at = pl.ds(pl.multiple_of(s * 256, 256), 256)
            got_scr[...] += dot(r1[:, at], jnp.concatenate(parts, axis=0))
            return 0

        lax.fori_loop(0, N // 2, planes, 0)

        for o, ref, m in ((0, r0, m0), (2, r2, m2), (1, None, None)):
            got = got_scr[...] if o == 1 else dot(ref[...], m[...])
            q_scr[o] = (got[:, :128] + got[:, 128:]) * wc[o]
        own_sum = send_sums(particle_sums(q_scr), e)

        for copy in lasts:
            copy.wait_recv()
        for o in range(3):
            if o == 1:
                table = own_last
            else:
                table = jnp.concatenate([lrecv[e, o // 2, 0:1, :], lrecv[e, o // 2, 1:2, :]], axis=1)
            hi, lo = split(table)
            table = jnp.concatenate(
                [jnp.broadcast_to(hi, (128, 256)), jnp.broadcast_to(lo, (128, 256))], axis=0
            )
            got = dot_t(sel[o], table)
            hi, lo = split((got[:, :128] + got[:, 128:]) * wc[o])
            vc[o, :, 0:128] = hi
            vc[o, :, 128:256] = lo
        to_voxels()

        def records(i, _):
            rows = pl.ds(pl.multiple_of(i * 128, 128), 128)
            b = back[rows, :].reshape(N, 8, 128)
            sums = [xn[f, i] + coupling[f] * b * inv[f, i] for f in range(2)]
            for f in range(2):
                xn[f, i] = sums[f]
            return 0

        lax.fori_loop(0, N, records, 0)
        for copy in halos[:4]:
            copy.wait_recv()
        for f in range(2):
            for d, at in ((0, 0), (1, N - 1)):
                xn[f, at] += cx[d, f] * hx[e, d, f]
            for d, at in ((0, 0), (1, N - 1)):
                xn[f, :, at] += cy[d, f] * hy[e, d, f]
        for copy in halos:
            copy.wait_send()

        @pl.when(t < ITERS - 1)
        def _():
            start_halos(xn, e + 1)

        if xn is xa:

            @pl.when(t == ITERS - 1)
            def _():
                for copy in outs:
                    copy.start()

        for copy in sum_copies(e):
            copy.wait_recv()
        y = yb[...]
        y = yrhs[...] + ydn[...] * pltpu.roll(y, 1, 0) + yup[...] * pltpu.roll(y, PACKED - 1, 0)
        yb[...] = y
        for g, row in ((0, 127), (1, 383)):
            sums = own_sum[:, 128 * g : 128 * g + 128] + srecv[e, 0, g : g + 1, :] + srecv[e, 1, g : g + 1, :]
            yb[row : row + 1, :] += gsurf[pl.ds(g, 1), :] * sums
        for copy in lasts + sum_copies(e):
            copy.wait_send()

        @pl.when(t < ITERS - 1)
        def _():
            start_lasts(e + 1)

    def two_iterations(u, _):
        iteration(2 * u, xa, xb)
        iteration(2 * u + 1, xb, xa)
        return 0

    lax.fori_loop(0, ITERS // 2, two_iterations, 0)

    for b in range(0, PACKED, 128):
        pack[:, b : b + 128] = jnp.transpose(yb[b : b + 128, :])
    for g, (base, rows) in enumerate(groups):
        for c in range(4):
            cls = 4 * g + c
            count = shell_counts[cls]
            start, end = shell_starts[cls], base + rows
            yo_ref[:, start : start + count] = pack[32 * c : 32 * c + 32, end - count : end]
    for copy in outs:
        copy.wait()


def shards(
    adjoint_rhs, conductance, phase, particle_rhs, diffusion_rate, exchange_rate,
    record_voxel, record_slot, record_weight,
):
    vmem = pl.BlockSpec(memory_space=pltpu.VMEM)
    hbm = pl.BlockSpec(memory_space=pltpu.HBM)
    free = pl.BlockSpec(memory_space=pl.ANY)
    field = (2, N, N, 8, 128)
    col = (8, 128)
    scratch = [
        pltpu.VMEM(field, F32),
        pltpu.VMEM(field[1:], F32),
        pltpu.VMEM(field[1:], jnp.int32),
        pltpu.VMEM((32, 1200), F32),
        pltpu.VMEM((8, 32), F32),
        pltpu.VMEM((8, 32), F32),
        pltpu.VMEM((3, 1, 512), jnp.int32),
        pltpu.VMEM((3, 1, 512), jnp.int32),
        pltpu.VMEM((3, 1, 512), F32),
        pltpu.VMEM((128, PACKED), F32),
        pltpu.VMEM(field, F32),
        pltpu.VMEM((2, N + 1, N, *col), F32),
        pltpu.VMEM(field, F32),
        pltpu.VMEM(field, F32),
        pltpu.VMEM(field, F32),
        pltpu.VMEM(field, F32),
        pltpu.VMEM(field, F32),
        pltpu.VMEM(field, F32),
        pltpu.VMEM((2, 2, N, *col), F32),
        pltpu.VMEM((5, 2, 2, N, *col), F32),
        pltpu.VMEM((5, 2, 2, N, *col), F32),
        pltpu.VMEM((5, 2, N, N, 128), F32),
        pltpu.VMEM((2, 2, N, *col), F32),
        pltpu.VMEM((2, 2, N, *col), F32),
        pltpu.VMEM((2048, 128), F32),
        pltpu.VMEM((512, 256), F32),
        pltpu.VMEM((512, 256), BF16),
        pltpu.VMEM((512, 256), BF16),
        pltpu.VMEM((512, 2048), BF16),
        pltpu.VMEM((512, 512), BF16),
        pltpu.VMEM((512, 512), BF16),
        pltpu.VMEM((2048, 512), BF16),
        pltpu.VMEM((512, 512), BF16),
        pltpu.VMEM((512, 512), BF16),
        pltpu.VMEM((3, 512, 256), BF16),
        pltpu.VMEM((3, 512, 128), F32),
        pltpu.VMEM((3, 512, 128), F32),
        pltpu.VMEM((3, 512, 256), BF16),
        pltpu.VMEM((2, N, N, 128), F32),
        pltpu.VMEM((128, 128), F32),
        pltpu.VMEM((128, 128), F32),
        pltpu.VMEM((PACKED, 128), F32),
        pltpu.VMEM((PACKED, 128), F32),
        pltpu.VMEM((PACKED, 128), F32),
        pltpu.VMEM((PACKED, 128), F32),
        pltpu.VMEM(col, F32),
        pltpu.VMEM(col, F32),
        pltpu.VMEM((5, 2, *col), F32),
        pltpu.VMEM((2, *col), F32),
        pltpu.VMEM((5, 2, *col), F32),
        pltpu.SemaphoreType.DMA((3, 8)),
        pltpu.SemaphoreType.DMA((6,)),
        pltpu.SemaphoreType.DMA((8,)),
        pltpu.SemaphoreType.DMA((5, 9)),
        pltpu.SemaphoreType.DMA((5, 9)),
    ]
    x, y = pl.pallas_call(
        kernel,
        out_shape=(
            pltpu.VMEM(adjoint_rhs.shape, F32),
            pltpu.VMEM((32, 1200), F32),
        ),
        in_specs=[hbm] * 9,
        out_specs=(free, vmem),
        scratch_shapes=scratch,
        compiler_params=pltpu.CompilerParams(
            collective_id=0, has_side_effects=True, vmem_limit_bytes=52 * 1024 * 1024
        ),
    )(
        adjoint_rhs,
        conductance,
        phase,
        particle_rhs.T,
        diffusion_rate,
        exchange_rate,
        record_voxel.reshape(3, 1, 512),
        record_slot.reshape(3, 1, 512),
        record_weight.reshape(3, 1, 512),
    )
    return x, y.T


def solution(mesh):
    grid = P("gx", "gy", "gz")
    parts = P(None, ("gx", "gy", "gz"))
    return jax.shard_map(
        shards,
        mesh=mesh,
        in_specs=(P(None, "gx", "gy", "gz"), grid, grid, parts, parts, parts, grid, grid, grid),
        out_specs=(P(None, "gx", "gy", "gz"), parts),
        check_vma=False,
    )
```
